32 devices in a mesh: gx: 16 (over z, x, core), gy: 2 (over y).
Axes of the slice: x: 2, y: 2, z: 4, core: 2. Of those that a mesh axis runs over, the one named last changes fastest.
Arguments:
- flow_populations: float32 [19, 32, 16, 256], P(None, 'gx', None, 'gy'), as said below
- heat_populations: float32 [7, 32, 16, 256], P(None, 'gx', None, 'gy'), as said below
- flow_weight: float32 [3, 32, 16, 256], P(None, 'gx', None, 'gy'), may hold values from -48 to 48
- heat_weight: float32 [32, 16, 256], P('gx', None, 'gy'), may hold values from -192 to 192
- resistance: float32 [32, 16, 256], P('gx', None, 'gy'), may hold values from 0.05 to 2
- conductivity: float32 [32, 16, 256], P('gx', None, 'gy'), may hold values from 0.5 to 2
- solid_mask: int32 [32, 16, 256], P('gx', None, 'gy'), may hold values 0 or 1
Outputs:
- resistance_sensitivity: float32 [32, 16, 256], P('gx', None, 'gy')
- conductivity_sensitivity: float32 [32, 16, 256], P('gx', None, 'gy')
The draws below stay inside these ranges and needn't reach their ends.
Inputs may be any that keep to these rules, and one draw needn't show every extreme that they name: `solid_mask`: 1 marks a solid voxel, 0 a fluid one. `flow_populations`: positive. `heat_populations`: positive.
All inputs are finite; a program needn't handle non-finite values. No bound on the sum of `solid_mask` on one device may be relied on, other than what follows from the above.
Results may differ from the reference program's by a relative error of at most 0.0003.
Values sent between devices are 32-bit elements; how exact they have to be, the bound alone decides.
A program may use at most 64 MiB of HBM per device.

```python
import math
import jax
import jax.numpy as jnp
import numpy as np
from jax import lax

STEPS = 3
CELLS_WIDTHWISE = 32
CELLS_DEPTHWISE = 256
CELLS_HEIGHTWISE = 16


def velocity_columns():
    velocity = np.array([[0, 0, 0], [1, 0, 0], [-1, 0, 0], [0, 1, 0], [0, -1, 0], [0, 0, 1], [0, 0, -1], [1, 1, 0], [-1, -1, 0], [1, -1, 0], [-1, 1, 0], [1, 0, 1], [-1, 0, -1], [1, 0, -1], [-1, 0, 1], [0, 1, 1], [0, -1, -1], [0, 1, -1], [0, -1, 1]], np.float32)
    weights = np.array([1.0 / 3.0] + [1.0 / 18.0] * 6 + [1.0 / 36.0] * 12, np.float32)
    return (velocity, weights)


def disturbance_grid(key, shape, spread):
    return spread * jax.random.truncated_normal(key, -3.0, 3.0, shape, jnp.float32)


def draw_flow_populations(key, part):
    key = jax.random.fold_in(key, 11)
    key_density, key_drift, key_noise = jax.random.split(key, 3)
    velocity, weights = velocity_columns()
    density = 1.0 + disturbance_grid(key_density, (CELLS_WIDTHWISE, CELLS_HEIGHTWISE, CELLS_DEPTHWISE), 0.05)
    drift = jnp.array([0.08, 0.03, 0.0], jnp.float32)[:, None, None, None] + disturbance_grid(key_drift, (3, CELLS_WIDTHWISE, CELLS_HEIGHTWISE, CELLS_DEPTHWISE), 0.03)
    chosen_heading = velocity[:, 0, None, None, None] * drift[0] + velocity[:, 1, None, None, None] * drift[1] + velocity[:, 2, None, None, None] * drift[2]
    kinetic = drift[0] * drift[0] + drift[1] * drift[1] + drift[2] * drift[2]
    balance = weights[:, None, None, None] * (density + 3.0 * chosen_heading + 4.5 * chosen_heading * chosen_heading - 1.5 * kinetic)
    stochastic_nudge = disturbance_grid(key_noise, (19, CELLS_WIDTHWISE, CELLS_HEIGHTWISE, CELLS_DEPTHWISE), 1.0)
    return balance * (1.0 + 0.1 * stochastic_nudge)


def draw_heat_populations(key, part):
    key = jax.random.fold_in(key, 23)
    tier_seed_handle, key_noise = jax.random.split(key, 2)
    energy_stencil_factors = np.array([0.25] + [0.125] * 6, np.float32)
    warmth_grid = 1.0 + disturbance_grid(tier_seed_handle, (CELLS_WIDTHWISE, CELLS_HEIGHTWISE, CELLS_DEPTHWISE), 0.1)
    stochastic_nudge = disturbance_grid(key_noise, (7, CELLS_WIDTHWISE, CELLS_HEIGHTWISE, CELLS_DEPTHWISE), 1.0)
    return energy_stencil_factors[:, None, None, None] * warmth_grid * (1.0 + 0.1 * stochastic_nudge)


def plant(result, rng, least, top_value):
    longest = result.shape.index(max(result.shape))
    spots = []
    for shift in (0, 1):
        where = [jax.random.randint(jax.random.fold_in(rng, axis), (), 0, length) for axis, length in enumerate(result.shape)]
        where[longest] = (where[longest] + shift) % result.shape[longest]
        spots.append(tuple(where))
    return result.at[spots[0]].set(least).at[spots[1]].set(top_value)


def steps_of(own_key, shape, shards, least, high):
    def one(position, parts):
        steps = jax.random.uniform(jax.random.fold_in(jax.random.fold_in(own_key, 6), position), (parts,), jnp.float32, least / len(shards), high / len(shards))
        return jnp.repeat(jnp.exp(steps), shape[position] // parts).reshape((-1,) + (1,) * (len(shape) - position - 1))

    gain = one(*shards[0])
    for cut in shards[1:]:
        gain = gain * one(*cut)
    return gain


def gaussian(stream_key, extent, width, limit, pieces=(), held_as=jnp.bfloat16):
    level = steps_of(stream_key, extent, pieces, -0.22, 0.18) if pieces else 1.0
    values = jax.random.normal(stream_key, extent, jnp.float32) * width * level
    return jnp.minimum(jnp.maximum(values, -limit), limit).astype(held_as)


def setup_inputs(seed: int = 0) -> dict:
    seeds = jax.random.split(jax.random.key(seed), 8)
    return {
        "flow_populations": draw_flow_populations(jax.random.fold_in(seeds[7], 71), 0),
        "heat_populations": draw_heat_populations(jax.random.fold_in(seeds[7], 71), 0),
        "flow_weight": gaussian(seeds[2], (3, CELLS_WIDTHWISE, CELLS_HEIGHTWISE, CELLS_DEPTHWISE), 8.0, 48.0, ((1, 16), (3, 2)), jnp.float32),
        "heat_weight": gaussian(seeds[3], (CELLS_WIDTHWISE, CELLS_HEIGHTWISE, CELLS_DEPTHWISE), 32.0, 192.0, ((0, 16), (2, 2)), jnp.float32),
        "resistance": jnp.clip(jnp.exp(math.log(2.0) - 3.6888794 * jax.random.uniform(seeds[4], (CELLS_WIDTHWISE, CELLS_HEIGHTWISE, CELLS_DEPTHWISE), jnp.float32) ** steps_of(seeds[4], (CELLS_WIDTHWISE, CELLS_HEIGHTWISE, CELLS_DEPTHWISE), ((0, 16), (2, 2)), -0.2, 0.2)), 0.05, 2.0),
        "conductivity": jnp.clip(jnp.exp(math.log(2.0) - 1.3862944 * jax.random.uniform(seeds[5], (CELLS_WIDTHWISE, CELLS_HEIGHTWISE, CELLS_DEPTHWISE), jnp.float32) ** steps_of(seeds[5], (CELLS_WIDTHWISE, CELLS_HEIGHTWISE, CELLS_DEPTHWISE), ((0, 16), (2, 2)), -0.2, 0.2)), 0.5, 2.0),
        "solid_mask": plant((jax.random.randint(seeds[6], (CELLS_WIDTHWISE, CELLS_HEIGHTWISE, CELLS_DEPTHWISE), 0, 3) < 1).astype(jnp.int32), jax.random.fold_in(seeds[6], 1), 0, 1),
    }


GHOST_RATE = 1.2
HEAT_RATE = 1.4

def lattice_tables():
    velocity = np.array([[0, 0, 0], [1, 0, 0], [-1, 0, 0], [0, 1, 0], [0, -1, 0], [0, 0, 1], [0, 0, -1], [1, 1, 0], [-1, -1, 0], [1, -1, 0], [-1, 1, 0], [1, 0, 1], [-1, 0, -1], [1, 0, -1], [-1, 0, 1], [0, 1, 1], [0, -1, -1], [0, 1, -1], [0, -1, 1]], np.int64)
    weights = np.array([1.0 / 3.0] + [1.0 / 18.0] * 6 + [1.0 / 36.0] * 12, np.float32)
    energy_stencil_factors = np.array([0.25] + [0.125] * 6, np.float32)
    dot_table = (velocity @ velocity.T).astype(np.float32)
    lengths = np.sum(velocity * velocity, axis=1).astype(np.float32)
    stress_map = (4.5 * weights[:, None] * (dot_table * dot_table - lengths[None, :] / 3.0)).astype(np.float32)
    flux_map = (4.0 * energy_stencil_factors[:, None] * dot_table[:7, :7]).astype(np.float32)
    opposite = np.array([0, 2, 1, 4, 3, 6, 5, 8, 7, 10, 9, 12, 11, 14, 13, 16, 15, 18, 17])
    return (velocity, weights, energy_stencil_factors, stress_map, flux_map, opposite)

def full_velocity():
    velocity = lattice_tables()[0]
    return np.concatenate([velocity, velocity[:7]], axis=0)

def collide(flow_part, energy_share, resistance, conductivity, solid_cells):
    velocity, weights, energy_stencil_factors, stress_map, flux_map, opposite = lattice_tables()
    highest = lax.Precision.HIGHEST
    vel_float = velocity.astype(np.float32)
    momentum = jnp.einsum('qa,qxzy->axzy', vel_float, flow_part, precision=highest)
    density = lax.optimization_barrier(jnp.sum(flow_part, axis=0))
    warmth_grid = lax.optimization_barrier(jnp.sum(energy_share, axis=0))
    fluid_cells = 1.0 - solid_cells
    velocity_field = momentum * (fluid_cells / (1.0 + resistance))
    chosen_heading = jnp.einsum('qa,axzy->qxzy', vel_float, velocity_field, precision=highest)
    kinetic = lax.optimization_barrier(jnp.sum(velocity_field * velocity_field, axis=0))
    equilibrium = weights[:, None, None, None] * (density + 3.0 * chosen_heading + 4.5 * chosen_heading * chosen_heading - 1.5 * kinetic)
    excess = flow_part - equilibrium
    stress = jnp.einsum('iq,qxzy->ixzy', stress_map, excess, precision=highest)
    momentum_diffusivity = 0.1 * jnp.exp(-2.0 * (warmth_grid - 1.0))
    shear_rate = 1.0 / (0.5 + 3.0 * momentum_diffusivity)
    relaxed = equilibrium + (1.0 - shear_rate) * stress + (1.0 - GHOST_RATE) * (excess - stress)
    bounced = flow_part[opposite]
    flow_post = solid_cells * bounced + fluid_cells * relaxed
    energy_balanced_populations = energy_stencil_factors[:, None, None, None] * warmth_grid * (1.0 + 4.0 * chosen_heading[:7])
    heat_excess = energy_share - energy_balanced_populations
    heat_flux = jnp.einsum('iq,qxzy->ixzy', flux_map, heat_excess, precision=highest)
    flux_rate = 1.0 / (0.5 + 0.4 * conductivity)
    heat_post = energy_balanced_populations + (1.0 - flux_rate) * heat_flux + (1.0 - HEAT_RATE) * (heat_excess - heat_flux)
    return (flow_post, heat_post)

def stream(lattice_state, direction):
    velocity_table = full_velocity() * direction
    shifted = []
    for member in range(velocity_table.shape[0]):
        step_x, step_y, step_z = (int(entry_value) for entry_value in velocity_table[member])
        shifted.append(jnp.roll(lattice_state[member], (step_x, step_z, step_y), axis=(0, 1, 2)))
    return jnp.stack(shifted)

def objective_seed(flow_weight, heat_weight):
    vel_float = lattice_tables()[0].astype(np.float32)
    flow_seed = jnp.einsum('qa,axzy->qxzy', vel_float, flow_weight, precision=lax.Precision.HIGHEST)
    heat_seed = jnp.broadcast_to(heat_weight[None], (7,) + heat_weight.shape)
    return jnp.concatenate([flow_seed, heat_seed], axis=0)

def reference(flow_populations, heat_populations, flow_weight, heat_weight, resistance, conductivity, solid_mask):
    solid_cells = solid_mask.astype(jnp.float32)
    lattice_state = jnp.concatenate([flow_populations, heat_populations], axis=0)
    history = []
    for section_index in range(STEPS):
        history.append(lattice_state)
        if section_index + 1 < STEPS:
            flow_post, heat_post = collide(lattice_state[:19], lattice_state[19:], resistance, conductivity, solid_cells)
            lattice_state = stream(jnp.concatenate([flow_post, heat_post], axis=0), 1)
    adjoint = objective_seed(flow_weight, heat_weight)
    resistance_sensitivity = jnp.zeros_like(resistance)
    conductivity_sensitivity = jnp.zeros_like(conductivity)

    def local_step(flow_part, energy_share, resist_field, conduct_field):
        return collide(flow_part, energy_share, resist_field, conduct_field, solid_cells)
    for section_index in reversed(range(STEPS)):
        arrived = stream(adjoint, -1)
        saved_state = history[section_index]
        unused, pullback = jax.vjp(local_step, saved_state[:19], saved_state[19:], resistance, conductivity)
        flow_back, heat_back, resist_back, conduct_back = pullback((arrived[:19], arrived[19:]))
        adjoint = jnp.concatenate([flow_back, heat_back], axis=0)
        resistance_sensitivity = resistance_sensitivity + resist_back
        conductivity_sensitivity = conductivity_sensitivity + conduct_back
    return (resistance_sensitivity, conductivity_sensitivity)
```

```python
import functools

import jax
import jax.numpy as jnp
from jax import lax
from jax.experimental import pallas as pl
from jax.experimental.pallas import tpu as pltpu
from jax.sharding import PartitionSpec as P

STEPS = 3
GHOST = 0.2
HEAT_GHOST = 0.4

FLOW = [
    (0, 0, 0), (1, 0, 0), (-1, 0, 0), (0, 1, 0), (0, -1, 0), (0, 0, 1), (0, 0, -1),
    (1, 1, 0), (-1, -1, 0), (1, -1, 0), (-1, 1, 0), (1, 0, 1), (-1, 0, -1),
    (1, 0, -1), (-1, 0, 1), (0, 1, 1), (0, -1, -1), (0, 1, -1), (0, -1, 1),
]
VELOCITY = FLOW + FLOW[:7]
MEMBERS = len(VELOCITY)
OPPOSITE = [0] + [q + 1 if q % 2 else q - 1 for q in range(1, 19)]
OPPOSITE = OPPOSITE + [19 + q for q in OPPOSITE[:7]]
ORDER = (
    [q for q in range(MEMBERS) if VELOCITY[q][0] == 1]
    + [q for q in range(MEMBERS) if VELOCITY[q][0] == -1]
    + [q for q in range(MEMBERS) if VELOCITY[q][0] == 0]
)
SLOT = [ORDER.index(q) for q in range(MEMBERS)]
FACE = sum(1 for q in range(MEMBERS) if VELOCITY[q][0] == 1)
UP = [q for q in range(MEMBERS) if VELOCITY[q][1] == 1]
DOWN = [q for q in range(MEMBERS) if VELOCITY[q][1] == -1]
ROUNDS = 5
FORWARD_0, SEED, FORWARD_1, BACK_2, BACK_1 = range(ROUNDS)
MESH = pl.DeviceIdType.MESH


def flow_moments(f):
    s = {q: f[q] + f[q + 1] for q in range(1, 19, 2)}
    d = {q: f[q] - f[q + 1] for q in range(1, 19, 2)}
    xy, xz, yz = s[7] + s[9], s[11] + s[13], s[15] + s[17]
    total = (f[0] + s[1] + s[3]) + (s[5] + xy) + (xz + yz)
    first = (
        (d[1] + d[7]) + (d[9] + d[11]) + d[13],
        (d[3] + d[7]) + (d[15] - d[9]) + d[17],
        (d[5] + d[11]) + (d[15] - d[13]) - d[17],
    )
    second = (
        s[1] + (xy + xz), s[3] + (xy + yz), s[5] + (xz + yz),
        s[7] - s[9], s[11] - s[13], s[15] - s[17],
    )
    return total, first, second


def spread(even, vector, tensor):
    x, y, z = vector
    xx, yy, zz, xy, xz, yz = tensor
    out = [even]

    def pair(e, o):
        out.append(e + o)
        out.append(e - o)

    ex, ey, ez = even + xx, even + yy, even + zz
    pair(ex, x)
    pair(ey, y)
    pair(ez, z)
    for e, cross, first, second in (
        (ex + yy, xy + xy, x, y), (ex + zz, xz + xz, x, z), (ey + zz, yz + yz, y, z)
    ):
        pair(e + cross, first + second)
        pair(e - cross, first - second)
    return out


def dot(a, b):
    return (a[0] * b[0] + a[1] * b[1]) + a[2] * b[2]


def state_moments(f, g, slow):
    density, momentum, second = flow_moments(f)
    third = density * (1.0 / 3.0)
    stress = tuple(m - third for m in second[:3]) + second[3:]
    u = tuple(slow * m for m in momentum)
    heat = (g[0] + (g[1] + g[2])) + ((g[3] + g[4]) + (g[5] + g[6]))
    flux = (g[1] - g[2], g[3] - g[4], g[5] - g[6])
    ease = jnp.exp(-2.0 * (heat - 1.0))
    omega = 1.0 / (0.5 + 0.3 * ease)
    return density, u, stress, heat, flux, omega, ease


def collide(f, g, solid, kappa, moments):
    density, u, stress, heat, flux, omega, _ = moments
    k_u, k_s = 4.5 * omega, 4.5 * (1.2 - omega)
    ku = tuple(k_u * m for m in u)
    tensor = (
        ku[0] * u[0] + k_s * stress[0], ku[1] * u[1] + k_s * stress[1],
        ku[2] * u[2] + k_s * stress[2], ku[0] * u[1] + k_s * stress[3],
        ku[0] * u[2] + k_s * stress[4], ku[1] * u[2] + k_s * stress[5],
    )
    even = 1.2 * density - (tensor[0] + tensor[1] + tensor[2]) * (1.0 / 3.0)
    vector = tuple(3.6 * m for m in u)
    w = 1.0 / 36.0
    relaxed = spread(
        w * even, tuple(w * m for m in vector), tuple(w * m for m in tensor)
    )
    out = []
    for q in range(19):
        scale = 12.0 if q == 0 else 2.0 if q < 7 else 1.0
        fluid = (relaxed[q] if scale == 1.0 else scale * relaxed[q]) - GHOST * f[q]
        out.append(jnp.where(solid, f[OPPOSITE[q]], fluid))
    sigma, pull = 1.4 - kappa, kappa * heat
    gate = tuple(0.5 * (pull * a + sigma * b) for a, b in zip(u, flux))
    base = (1.4 / 8.0) * heat
    out.append(2.0 * base - HEAT_GHOST * g[0])
    for axis in range(3):
        a, b = g[1 + 2 * axis], g[2 + 2 * axis]
        out.append((base + gate[axis]) - HEAT_GHOST * a)
        out.append((base - gate[axis]) - HEAT_GHOST * b)
    return out


def adjoint_sums(l, m, fluid):
    weighted = [12.0 * l[0]] + [2.0 * v for v in l[1:7]] + list(l[7:19])
    even, vector, tensor = flow_moments(weighted)
    scale = fluid * (1.0 / 36.0)
    even = scale * even
    vector = tuple(scale * v for v in vector)
    third = even * (1.0 / 3.0)
    tensor = tuple(scale * v - third for v in tensor[:3]) + tuple(scale * v for v in tensor[3:])
    gate = tuple(0.5 * (m[1 + 2 * k] - m[2 + 2 * k]) for k in range(3))
    return even, vector, tensor, gate


def sensitivities(sums, u, heat, flux, omega, kappa):
    _, vector, (xx, yy, zz, xy, xz, yz), gate = sums
    bent = (
        (xx * u[0] + xy * u[1]) + xz * u[2],
        (xy * u[0] + yy * u[1]) + yz * u[2],
        (xz * u[0] + yz * u[1]) + zz * u[2],
    )
    k_u, pull = 9.0 * omega, kappa * heat
    back = tuple(k_u * b + (3.6 * v + pull * e) for b, v, e in zip(bent, vector, gate))
    resist = dot(u, back)
    conduct = dot(gate, tuple(heat * a - b for a, b in zip(u, flux)))
    return back, bent, resist, conduct


def collide_back(l, m, sums, moments, back, bent, solid, slow, kappa):
    even, vector, tensor, gate = sums
    _, u, stress, heat, flux, omega, ease = moments
    xx, yy, zz, xy, xz, yz = tensor
    cross = xy * stress[3] + xz * stress[4] + yz * stress[5]
    inner = (xx * stress[0] + yy * stress[1]) + (zz * stress[2] + (cross + cross))
    omega_back = 4.5 * (dot(u, bent) - inner)
    k_s = 4.5 * (1.2 - omega)
    stress_back = tuple(k_s * t for t in tensor)
    density_back = 1.2 * even - (stress_back[0] + stress_back[1] + stress_back[2]) * (1.0 / 3.0)
    momentum_back = tuple(slow * b for b in back)
    smooth = spread(density_back, momentum_back, stress_back)
    out = []
    for q in range(19):
        out.append(jnp.where(solid, l[OPPOSITE[q]], -GHOST * l[q]) + smooth[q])
    moved = (m[0] + m[0] + (m[1] + m[2])) + ((m[3] + m[4]) + (m[5] + m[6]))
    heat_back = (1.4 / 8.0) * moved + kappa * dot(gate, u) + omega_back * (0.6 * ease) * (omega * omega)
    sigma = 1.4 - kappa
    flux_back = tuple(sigma * e for e in gate)
    out.append(heat_back - HEAT_GHOST * m[0])
    for axis in range(3):
        a, b = m[1 + 2 * axis], m[2 + 2 * axis]
        out.append((heat_back + flux_back[axis]) - HEAT_GHOST * a)
        out.append((heat_back - flux_back[axis]) - HEAT_GHOST * b)
    return out


def kernel(
    gx, gy, flow_ref, heat_ref, flow_w_ref, heat_w_ref, resist_ref, conduct_ref, solid_ref,
    resist_out, conduct_out,
    ext, own_edge, edge, saved, fields, send_sem, recv_sem,
):
    width, height, depth = resist_ref.shape
    sides = edge.shape[1]
    me_x, me_y = lax.axis_index("gx"), lax.axis_index("gy")
    right, left = lax.rem(me_x + 1, gx), lax.rem(me_x + gx - 1, gx)
    up, down = lax.rem(me_y + 1, gy), lax.rem(me_y + gy - 1, gy)
    columns = [(up, 0)] if sides == 1 else [(up, 0), (down, 1)]

    barrier = pltpu.get_barrier_semaphore()
    partners = [(right, me_y), (left, me_y)]
    for y, _ in columns:
        partners += [(me_x, y), (right, y), (left, y)]
    for partner in partners:
        pl.semaphore_signal(barrier, inc=1, device_id=partner, device_id_type=MESH)

    lane = lax.broadcasted_iota(jnp.int32, (height, depth), 1)

    def copies(r):
        made = []

        def add(src, dst, device):
            k = len(made)
            made.append(
                pltpu.make_async_remote_copy(
                    src_ref=src, dst_ref=dst,
                    send_sem=send_sem.at[r, k], recv_sem=recv_sem.at[r, k],
                    device_id=device, device_id_type=MESH,
                )
            )

        for y, side in columns:
            add(own_edge.at[r, width - 1], edge.at[r, side, 0], (right, y))
            add(own_edge.at[r, 0], edge.at[r, side, width + 1], (left, y))
        add(ext.at[r, width, pl.ds(0, FACE)], ext.at[r, 0, pl.ds(0, FACE)], (right, me_y))
        add(ext.at[r, 1, pl.ds(FACE, FACE)], ext.at[r, width + 1, pl.ds(FACE, FACE)], (left, me_y))
        for y, side in columns:
            add(own_edge.at[r], edge.at[r, side, pl.ds(1, width)], (me_x, y))
        return made

    def start(r):
        for copy in copies(r):
            copy.start()

    def arrive(r):
        for copy in copies(r):
            copy.wait_recv()

    def leave(r, x, members):
        packed = None
        for q in range(MEMBERS):
            if members[q] is None:
                continue
            value = members[q]
            _, step_y, step_z = VELOCITY[q]
            if step_z:
                value = pltpu.roll(value, step_z % height, 0)
            if step_y:
                value = pltpu.roll(value, step_y % depth, 1)
            ext[r, x + 1, SLOT[q]] = value
            if step_y:
                place = UP.index(q) if step_y == 1 else DOWN.index(q)
                shift = place * step_y % depth
                where = place if step_y == 1 else depth - 1 - place
                turned = pltpu.roll(value, shift, 1) if shift else value
                packed = turned if packed is None else jnp.where(lane == where, turned, packed)
        own_edge[r, x] = packed

    def gather(r, x, q):
        step_x, step_y, _ = VELOCITY[q]
        value = ext[r, x + 1 - step_x, SLOT[q]]
        if step_y:
            side = 0 if step_y == 1 else sides - 1
            packed = edge[r, side, x + 1 - step_x]
            place = UP.index(q) if step_y == 1 else DOWN.index(q)
            shift = -place * step_y % depth
            turned = pltpu.roll(packed, shift, 1) if shift else packed
            value = jnp.where(lane == (0 if step_y == 1 else depth - 1), turned, value)
        return value

    def keep(t, x, moments):
        _, u, stress, heat, flux, omega, ease = moments
        for k, value in enumerate((*u, heat, *flux, omega, ease, *stress)):
            saved[t, x, k] = value

    def kept(t, x, whole):
        values = [saved[t, x, k] for k in range(15 if whole else 8)]
        return (
            None, tuple(values[:3]), tuple(values[9:15]) if whole else None, values[3],
            tuple(values[4:7]), values[7], values[8] if whole else None,
        )

    def planes(body):
        def step(x, carry):
            body(x)
            return carry

        lax.fori_loop(0, width, step, 0)

    def first(x):
        solid = solid_ref[x] != 0
        slow = jnp.where(solid, 0.0, 1.0) / (1.0 + resist_ref[x])
        kappa = 1.0 / (0.5 + 0.4 * conduct_ref[x])
        fields[x, 0] = slow
        fields[x, 1] = kappa
        f = [flow_ref[q, x] for q in range(19)]
        g = [heat_ref[q, x] for q in range(7)]
        moments = state_moments(f, g, slow)
        keep(0, x, moments)
        leave(FORWARD_0, x, collide(f, g, solid, kappa, moments))

    planes(first)
    pl.semaphore_wait(barrier, len(partners))
    start(FORWARD_0)

    def seed(x):
        weights = [flow_w_ref[k, x] for k in range(3)]
        heat = heat_w_ref[x]
        members = [None] * MEMBERS
        for q in range(MEMBERS):
            if q >= 19:
                members[OPPOSITE[q]] = heat
            elif q:
                value = None
                for weight, step in zip(weights, VELOCITY[q]):
                    if step:
                        term = weight if step == 1 else -weight
                        value = term if value is None else value + term
                members[OPPOSITE[q]] = value
        leave(SEED, x, members)

    planes(seed)
    start(SEED)

    def second(x):
        solid, slow, kappa = solid_ref[x] != 0, fields[x, 0], fields[x, 1]
        state = [gather(FORWARD_0, x, q) for q in range(MEMBERS)]
        f, g = state[:19], state[19:]
        moments = state_moments(f, g, slow)
        keep(1, x, moments)
        leave(FORWARD_1, x, collide(f, g, solid, kappa, moments))

    arrive(FORWARD_0)
    planes(second)
    start(FORWARD_1)

    def reverse(r, x, moments, target):
        solid, slow, kappa = solid_ref[x] != 0, fields[x, 0], fields[x, 1]
        back = [
            jnp.zeros((height, depth), jnp.float32) if r == SEED and q == 0
            else gather(r, x, OPPOSITE[q])
            for q in range(MEMBERS)
        ]
        l, m = back[:19], back[19:]
        sums = adjoint_sums(l, m, jnp.where(solid, 0.0, 1.0))
        _, u, _, heat, flux, omega, _ = moments
        u_back, bent, resist, conduct = sensitivities(sums, u, heat, flux, omega, kappa)
        if r == SEED:
            resist_out[x] = resist
            conduct_out[x] = conduct
        elif target is not None:
            resist_out[x] += resist
            conduct_out[x] += conduct
        else:
            resist_out[x] = -(resist_out[x] + resist) / (1.0 + resist_ref[x])
            conduct_out[x] = (conduct_out[x] + conduct) * (-0.4 * kappa * kappa)
        if target is not None:
            out = collide_back(l, m, sums, moments, u_back, bent, solid, slow, kappa)
            leave(target, x, [out[OPPOSITE[q]] for q in range(MEMBERS)])

    def third(x):
        state = [gather(FORWARD_1, x, q) for q in range(MEMBERS)]
        reverse(SEED, x, state_moments(state[:19], state[19:], fields[x, 0]), BACK_2)

    arrive(SEED)
    arrive(FORWARD_1)
    planes(third)
    start(BACK_2)

    arrive(BACK_2)
    planes(lambda x: reverse(BACK_2, x, kept(1, x, True), BACK_1))
    start(BACK_1)

    arrive(BACK_1)
    planes(lambda x: reverse(BACK_1, x, kept(0, x, False), None))

    for r in range(ROUNDS):
        for copy in copies(r):
            copy.wait_send()


def on_device(gx, gy, flow, heat, flow_weight, heat_weight, resistance, conductivity, solid_mask):
    shape = resistance.shape
    width, height, depth = shape
    sides = 1 if gy == 2 else 2
    count = 2 + 3 * sides
    block = pl.BlockSpec(memory_space=pltpu.VMEM)
    return pl.pallas_call(
        functools.partial(kernel, gx, gy),
        out_shape=[jax.ShapeDtypeStruct(shape, jnp.float32)] * 2,
        in_specs=[block] * 7,
        out_specs=[block] * 2,
        scratch_shapes=[
            pltpu.VMEM((ROUNDS, width + 2, MEMBERS, height, depth), jnp.float32),
            pltpu.VMEM((ROUNDS, width, height, depth), jnp.float32),
            pltpu.VMEM((ROUNDS, sides, width + 2, height, depth), jnp.float32),
            pltpu.VMEM((STEPS - 1, width, 15, height, depth), jnp.float32),
            pltpu.VMEM((width, 2, height, depth), jnp.float32),
            pltpu.SemaphoreType.DMA((ROUNDS, count)),
            pltpu.SemaphoreType.DMA((ROUNDS, count)),
        ],
        compiler_params=pltpu.CompilerParams(
            collective_id=0, has_side_effects=True, vmem_limit_bytes=32 * 1024 * 1024
        ),
    )(flow, heat, flow_weight, heat_weight, resistance, conductivity, solid_mask)


def solution(mesh):
    wide, flat = P(None, "gx", None, "gy"), P("gx", None, "gy")
    return jax.shard_map(
        functools.partial(on_device, mesh.shape["gx"], mesh.shape["gy"]),
        mesh=mesh,
        in_specs=(wide, wide, wide, flat, flat, flat, flat),
        out_specs=(flat, flat),
        check_vma=False,
    )
```

```python
import functools

import jax
import jax.numpy as jnp
from jax import lax
from jax.experimental import pallas as pl
from jax.experimental.pallas import tpu as pltpu
from jax.sharding import PartitionSpec as P

STEPS = 3
GHOST = 0.2
HEAT_GHOST = 0.4

FLOW = [
    (0, 0, 0), (1, 0, 0), (-1, 0, 0), (0, 1, 0), (0, -1, 0), (0, 0, 1), (0, 0, -1),
    (1, 1, 0), (-1, -1, 0), (1, -1, 0), (-1, 1, 0), (1, 0, 1), (-1, 0, -1),
    (1, 0, -1), (-1, 0, 1), (0, 1, 1), (0, -1, -1), (0, 1, -1), (0, -1, 1),
]
VELOCITY = FLOW + FLOW[:7]
MEMBERS = len(VELOCITY)
OPPOSITE = [0] + [q + 1 if q % 2 else q - 1 for q in range(1, 19)]
OPPOSITE = OPPOSITE + [19 + q for q in OPPOSITE[:7]]
ORDER = (
    [q for q in range(MEMBERS) if VELOCITY[q][0] == 1]
    + [q for q in range(MEMBERS) if VELOCITY[q][0] == -1]
    + [q for q in range(MEMBERS) if VELOCITY[q][0] == 0]
)
SLOT = [ORDER.index(q) for q in range(MEMBERS)]
FACE = sum(1 for q in range(MEMBERS) if VELOCITY[q][0] == 1)
UP = [q for q in range(MEMBERS) if VELOCITY[q][1] == 1]
DOWN = [q for q in range(MEMBERS) if VELOCITY[q][1] == -1]
ROUNDS = 5
FORWARD_0, SEED, FORWARD_1, BACK_2, BACK_1 = range(ROUNDS)
MESH = pl.DeviceIdType.MESH


def flow_moments(f):
    s = {q: f[q] + f[q + 1] for q in range(1, 19, 2)}
    d = {q: f[q] - f[q + 1] for q in range(1, 19, 2)}
    xy, xz, yz = s[7] + s[9], s[11] + s[13], s[15] + s[17]
    total = (f[0] + s[1] + s[3]) + (s[5] + xy) + (xz + yz)
    first = (
        (d[1] + d[7]) + (d[9] + d[11]) + d[13],
        (d[3] + d[7]) + (d[15] - d[9]) + d[17],
        (d[5] + d[11]) + (d[15] - d[13]) - d[17],
    )
    second = (
        s[1] + (xy + xz), s[3] + (xy + yz), s[5] + (xz + yz),
        s[7] - s[9], s[11] - s[13], s[15] - s[17],
    )
    return total, first, second


def spread(even, vector, tensor):
    x, y, z = vector
    xx, yy, zz, xy, xz, yz = tensor
    out = [even]

    def pair(e, o):
        out.append(e + o)
        out.append(e - o)

    ex, ey, ez = even + xx, even + yy, even + zz
    pair(ex, x)
    pair(ey, y)
    pair(ez, z)
    for e, cross, first, second in (
        (ex + yy, xy + xy, x, y), (ex + zz, xz + xz, x, z), (ey + zz, yz + yz, y, z)
    ):
        pair(e + cross, first + second)
        pair(e - cross, first - second)
    return out


def dot(a, b):
    return (a[0] * b[0] + a[1] * b[1]) + a[2] * b[2]


def state_moments(f, g, slow):
    density, momentum, second = flow_moments(f)
    third = density * (1.0 / 3.0)
    stress = tuple(m - third for m in second[:3]) + second[3:]
    u = tuple(slow * m for m in momentum)
    heat = (g[0] + (g[1] + g[2])) + ((g[3] + g[4]) + (g[5] + g[6]))
    flux = (g[1] - g[2], g[3] - g[4], g[5] - g[6])
    ease = jnp.exp(-2.0 * (heat - 1.0))
    omega = 1.0 / (0.5 + 0.3 * ease)
    return density, u, stress, heat, flux, omega, ease


def collide(f, g, solid, kappa, moments):
    density, u, stress, heat, flux, omega, _ = moments
    k_u, k_s = 4.5 * omega, 4.5 * (1.2 - omega)
    ku = tuple(k_u * m for m in u)
    tensor = (
        ku[0] * u[0] + k_s * stress[0], ku[1] * u[1] + k_s * stress[1],
        ku[2] * u[2] + k_s * stress[2], ku[0] * u[1] + k_s * stress[3],
        ku[0] * u[2] + k_s * stress[4], ku[1] * u[2] + k_s * stress[5],
    )
    even = 1.2 * density - (tensor[0] + tensor[1] + tensor[2]) * (1.0 / 3.0)
    vector = tuple(3.6 * m for m in u)
    w = 1.0 / 36.0
    relaxed = spread(
        w * even, tuple(w * m for m in vector), tuple(w * m for m in tensor)
    )
    out = []
    for q in range(19):
        scale = 12.0 if q == 0 else 2.0 if q < 7 else 1.0
        fluid = (relaxed[q] if scale == 1.0 else scale * relaxed[q]) - GHOST * f[q]
        out.append(jnp.where(solid, f[OPPOSITE[q]], fluid))
    sigma, pull = 1.4 - kappa, kappa * heat
    gate = tuple(0.5 * (pull * a + sigma * b) for a, b in zip(u, flux))
    base = (1.4 / 8.0) * heat
    out.append(2.0 * base - HEAT_GHOST * g[0])
    for axis in range(3):
        a, b = g[1 + 2 * axis], g[2 + 2 * axis]
        out.append((base + gate[axis]) - HEAT_GHOST * a)
        out.append((base - gate[axis]) - HEAT_GHOST * b)
    return out


def adjoint_sums(l, m, fluid):
    weighted = [12.0 * l[0]] + [2.0 * v for v in l[1:7]] + list(l[7:19])
    even, vector, tensor = flow_moments(weighted)
    scale = fluid * (1.0 / 36.0)
    even = scale * even
    vector = tuple(scale * v for v in vector)
    third = even * (1.0 / 3.0)
    tensor = tuple(scale * v - third for v in tensor[:3]) + tuple(scale * v for v in tensor[3:])
    gate = tuple(0.5 * (m[1 + 2 * k] - m[2 + 2 * k]) for k in range(3))
    return even, vector, tensor, gate


def sensitivities(sums, u, heat, flux, omega, kappa):
    _, vector, (xx, yy, zz, xy, xz, yz), gate = sums
    bent = (
        (xx * u[0] + xy * u[1]) + xz * u[2],
        (xy * u[0] + yy * u[1]) + yz * u[2],
        (xz * u[0] + yz * u[1]) + zz * u[2],
    )
    k_u, pull = 9.0 * omega, kappa * heat
    back = tuple(k_u * b + (3.6 * v + pull * e) for b, v, e in zip(bent, vector, gate))
    resist = dot(u, back)
    conduct = dot(gate, tuple(heat * a - b for a, b in zip(u, flux)))
    return back, bent, resist, conduct


def collide_back(l, m, sums, moments, back, bent, solid, slow, kappa):
    even, vector, tensor, gate = sums
    _, u, stress, heat, flux, omega, ease = moments
    xx, yy, zz, xy, xz, yz = tensor
    cross = xy * stress[3] + xz * stress[4] + yz * stress[5]
    inner = (xx * stress[0] + yy * stress[1]) + (zz * stress[2] + (cross + cross))
    omega_back = 4.5 * (dot(u, bent) - inner)
    k_s = 4.5 * (1.2 - omega)
    stress_back = tuple(k_s * t for t in tensor)
    density_back = 1.2 * even - (stress_back[0] + stress_back[1] + stress_back[2]) * (1.0 / 3.0)
    momentum_back = tuple(slow * b for b in back)
    smooth = spread(density_back, momentum_back, stress_back)
    out = []
    for q in range(19):
        out.append(jnp.where(solid, l[OPPOSITE[q]], -GHOST * l[q]) + smooth[q])
    moved = (m[0] + m[0] + (m[1] + m[2])) + ((m[3] + m[4]) + (m[5] + m[6]))
    heat_back = (1.4 / 8.0) * moved + kappa * dot(gate, u) + omega_back * (0.6 * ease) * (omega * omega)
    sigma = 1.4 - kappa
    flux_back = tuple(sigma * e for e in gate)
    out.append(heat_back - HEAT_GHOST * m[0])
    for axis in range(3):
        a, b = m[1 + 2 * axis], m[2 + 2 * axis]
        out.append((heat_back + flux_back[axis]) - HEAT_GHOST * a)
        out.append((heat_back - flux_back[axis]) - HEAT_GHOST * b)
    return out


def kernel(
    gx, gy, *refs
):
    whole, (resist_out, conduct_out), inputs = refs[:7], refs[7:9], refs[9:16]
    flow_ref, heat_ref, resist_ref, conduct_ref, solid_ref, flow_w_ref, heat_w_ref = inputs
    ext, own_edge, edge, saved, fields, load_sem, send_sem, recv_sem = refs[16:]
    width, height, depth = resist_ref.shape
    sides = edge.shape[1]
    me_x, me_y = lax.axis_index("gx"), lax.axis_index("gy")
    right, left = lax.rem(me_x + 1, gx), lax.rem(me_x + gx - 1, gx)
    up, down = lax.rem(me_y + 1, gy), lax.rem(me_y + gy - 1, gy)
    columns = [(up, 0)] if sides == 1 else [(up, 0), (down, 1)]

    loads = [
        pltpu.make_async_copy(src, dst, load_sem.at[k])
        for k, (src, dst) in enumerate(zip(whole, inputs))
    ]
    for load in loads:
        load.start()

    barrier = pltpu.get_barrier_semaphore()
    partners = [(right, me_y), (left, me_y)]
    for y, _ in columns:
        partners += [(me_x, y), (right, y), (left, y)]
    for partner in partners:
        pl.semaphore_signal(barrier, inc=1, device_id=partner, device_id_type=MESH)

    lane = lax.broadcasted_iota(jnp.int32, (height, depth), 1)

    def copies(r):
        made = []

        def add(src, dst, device):
            k = len(made)
            made.append(
                pltpu.make_async_remote_copy(
                    src_ref=src, dst_ref=dst,
                    send_sem=send_sem.at[r, k], recv_sem=recv_sem.at[r, k],
                    device_id=device, device_id_type=MESH,
                )
            )

        for y, side in columns:
            add(own_edge.at[r, width - 1], edge.at[r, side, 0], (right, y))
            add(own_edge.at[r, 0], edge.at[r, side, width + 1], (left, y))
        add(ext.at[r, width, pl.ds(0, FACE)], ext.at[r, 0, pl.ds(0, FACE)], (right, me_y))
        add(ext.at[r, 1, pl.ds(FACE, FACE)], ext.at[r, width + 1, pl.ds(FACE, FACE)], (left, me_y))
        for y, side in columns:
            add(own_edge.at[r], edge.at[r, side, pl.ds(1, width)], (me_x, y))
        return made

    def start(r):
        for copy in copies(r):
            copy.start()

    def arrive(r):
        for copy in copies(r):
            copy.wait_recv()

    def leave(r, x, members):
        packed = None
        for q in range(MEMBERS):
            if members[q] is None:
                continue
            value = members[q]
            _, step_y, step_z = VELOCITY[q]
            if step_z:
                value = pltpu.roll(value, step_z % height, 0)
            if step_y:
                value = pltpu.roll(value, step_y % depth, 1)
            ext[r, x + 1, SLOT[q]] = value
            if step_y:
                place = UP.index(q) if step_y == 1 else DOWN.index(q)
                shift = place * step_y % depth
                where = place if step_y == 1 else depth - 1 - place
                turned = pltpu.roll(value, shift, 1) if shift else value
                packed = turned if packed is None else jnp.where(lane == where, turned, packed)
        own_edge[r, x] = packed

    def gather(r, x, q):
        step_x, step_y, _ = VELOCITY[q]
        value = ext[r, x + 1 - step_x, SLOT[q]]
        if step_y:
            side = 0 if step_y == 1 else sides - 1
            packed = edge[r, side, x + 1 - step_x]
            place = UP.index(q) if step_y == 1 else DOWN.index(q)
            shift = -place * step_y % depth
            turned = pltpu.roll(packed, shift, 1) if shift else packed
            value = jnp.where(lane == (0 if step_y == 1 else depth - 1), turned, value)
        return value

    def keep(t, x, moments):
        _, u, stress, heat, flux, omega, ease = moments
        for k, value in enumerate((*u, heat, *flux, omega, ease, *stress)):
            saved[t, x, k] = value

    def kept(t, x, whole):
        values = [saved[t, x, k] for k in range(15 if whole else 8)]
        return (
            None, tuple(values[:3]), tuple(values[9:15]) if whole else None, values[3],
            tuple(values[4:7]), values[7], values[8] if whole else None,
        )

    def planes(body):
        def step(x, carry):
            body(x)
            return carry

        lax.fori_loop(0, width, step, 0)

    def first(x):
        solid = solid_ref[x] != 0
        slow = jnp.where(solid, 0.0, 1.0) / (1.0 + resist_ref[x])
        kappa = 1.0 / (0.5 + 0.4 * conduct_ref[x])
        fields[x, 0] = slow
        fields[x, 1] = kappa
        f = [flow_ref[q, x] for q in range(19)]
        g = [heat_ref[q, x] for q in range(7)]
        moments = state_moments(f, g, slow)
        keep(0, x, moments)
        leave(FORWARD_0, x, collide(f, g, solid, kappa, moments))

    for load in loads[:5]:
        load.wait()
    planes(first)
    pl.semaphore_wait(barrier, len(partners))
    start(FORWARD_0)

    def seed(x):
        weights = [flow_w_ref[k, x] for k in range(3)]
        heat = heat_w_ref[x]
        members = [None] * MEMBERS
        for q in range(MEMBERS):
            if q >= 19:
                members[OPPOSITE[q]] = heat
            elif q:
                value = None
                for weight, step in zip(weights, VELOCITY[q]):
                    if step:
                        term = weight if step == 1 else -weight
                        value = term if value is None else value + term
                members[OPPOSITE[q]] = value
        leave(SEED, x, members)

    for load in loads[5:]:
        load.wait()
    planes(seed)
    start(SEED)

    def second(x):
        solid, slow, kappa = solid_ref[x] != 0, fields[x, 0], fields[x, 1]
        state = [gather(FORWARD_0, x, q) for q in range(MEMBERS)]
        f, g = state[:19], state[19:]
        moments = state_moments(f, g, slow)
        keep(1, x, moments)
        leave(FORWARD_1, x, collide(f, g, solid, kappa, moments))

    arrive(FORWARD_0)
    planes(second)
    start(FORWARD_1)

    def reverse(r, x, moments, target):
        solid, slow, kappa = solid_ref[x] != 0, fields[x, 0], fields[x, 1]
        back = [
            jnp.zeros((height, depth), jnp.float32) if r == SEED and q == 0
            else gather(r, x, OPPOSITE[q])
            for q in range(MEMBERS)
        ]
        l, m = back[:19], back[19:]
        sums = adjoint_sums(l, m, jnp.where(solid, 0.0, 1.0))
        _, u, _, heat, flux, omega, _ = moments
        u_back, bent, resist, conduct = sensitivities(sums, u, heat, flux, omega, kappa)
        if r == SEED:
            resist_out[x] = resist
            conduct_out[x] = conduct
        elif target is not None:
            resist_out[x] += resist
            conduct_out[x] += conduct
        else:
            resist_out[x] = -(resist_out[x] + resist) / (1.0 + resist_ref[x])
            conduct_out[x] = (conduct_out[x] + conduct) * (-0.4 * kappa * kappa)
        if target is not None:
            out = collide_back(l, m, sums, moments, u_back, bent, solid, slow, kappa)
            leave(target, x, [out[OPPOSITE[q]] for q in range(MEMBERS)])

    def third(x):
        state = [gather(FORWARD_1, x, q) for q in range(MEMBERS)]
        reverse(SEED, x, state_moments(state[:19], state[19:], fields[x, 0]), BACK_2)

    arrive(SEED)
    arrive(FORWARD_1)
    planes(third)
    start(BACK_2)

    arrive(BACK_2)
    planes(lambda x: reverse(BACK_2, x, kept(1, x, True), BACK_1))
    start(BACK_1)

    arrive(BACK_1)
    planes(lambda x: reverse(BACK_1, x, kept(0, x, False), None))

    for r in range(ROUNDS):
        for copy in copies(r):
            copy.wait_send()


def write_out(resist_ref, conduct_ref, resist_out, conduct_out, sem):
    stores = [
        pltpu.make_async_copy(resist_ref, resist_out, sem.at[0]),
        pltpu.make_async_copy(conduct_ref, conduct_out, sem.at[1]),
    ]
    for store in stores:
        store.start()
    for store in stores:
        store.wait()


def on_device(gx, gy, flow, heat, flow_weight, heat_weight, resistance, conductivity, solid_mask):
    shape = resistance.shape
    width, height, depth = shape
    sides = 1 if gy == 2 else 2
    count = 2 + 3 * sides
    args = (flow, heat, resistance, conductivity, solid_mask, flow_weight, heat_weight)
    far = pl.BlockSpec(memory_space=pltpu.HBM)
    near = pl.BlockSpec(memory_space=pltpu.VMEM)
    result = [jax.ShapeDtypeStruct(shape, jnp.float32)] * 2
    found = pl.pallas_call(
        functools.partial(kernel, gx, gy),
        out_shape=result,
        in_specs=[far] * len(args),
        out_specs=[near] * 2,
        scratch_shapes=[pltpu.VMEM(a.shape, a.dtype) for a in args] + [
            pltpu.VMEM((ROUNDS, width + 2, MEMBERS, height, depth), jnp.float32),
            pltpu.VMEM((ROUNDS, width, height, depth), jnp.float32),
            pltpu.VMEM((ROUNDS, sides, width + 2, height, depth), jnp.float32),
            pltpu.VMEM((STEPS - 1, width, 15, height, depth), jnp.float32),
            pltpu.VMEM((width, 2, height, depth), jnp.float32),
            pltpu.SemaphoreType.DMA((len(args),)),
            pltpu.SemaphoreType.DMA((ROUNDS, count)),
            pltpu.SemaphoreType.DMA((ROUNDS, count)),
        ],
        compiler_params=pltpu.CompilerParams(
            collective_id=0, has_side_effects=True, vmem_limit_bytes=64 * 1024 * 1024
        ),
    )(*args)
    return pl.pallas_call(
        write_out,
        out_shape=result,
        in_specs=[far] * 2,
        out_specs=[far] * 2,
        scratch_shapes=[pltpu.SemaphoreType.DMA((2,))],
        compiler_params=pltpu.CompilerParams(vmem_limit_bytes=64 * 1024 * 1024),
    )(*found)


def solution(mesh):
    wide, flat = P(None, "gx", None, "gy"), P("gx", None, "gy")
    return jax.shard_map(
        functools.partial(on_device, mesh.shape["gx"], mesh.shape["gy"]),
        mesh=mesh,
        in_specs=(wide, wide, wide, flat, flat, flat, flat),
        out_specs=(flat, flat),
        check_vma=False,
    )
```

```python
import functools

import jax
import jax.numpy as jnp
from jax import lax
from jax.experimental import pallas as pl
from jax.experimental.pallas import tpu as pltpu
from jax.sharding import PartitionSpec as P

STEPS = 3
GHOST = 0.2
HEAT_GHOST = 0.4

FLOW = [
    (0, 0, 0), (1, 0, 0), (-1, 0, 0), (0, 1, 0), (0, -1, 0), (0, 0, 1), (0, 0, -1),
    (1, 1, 0), (-1, -1, 0), (1, -1, 0), (-1, 1, 0), (1, 0, 1), (-1, 0, -1),
    (1, 0, -1), (-1, 0, 1), (0, 1, 1), (0, -1, -1), (0, 1, -1), (0, -1, 1),
]
VELOCITY = FLOW + FLOW[:7]
MEMBERS = len(VELOCITY)
OPPOSITE = [0] + [q + 1 if q % 2 else q - 1 for q in range(1, 19)]
OPPOSITE = OPPOSITE + [19 + q for q in OPPOSITE[:7]]
ORDER = (
    [q for q in range(MEMBERS) if VELOCITY[q][0] == 1]
    + [q for q in range(MEMBERS) if VELOCITY[q][0] == -1]
    + [q for q in range(MEMBERS) if VELOCITY[q][0] == 0]
)
SLOT = [ORDER.index(q) for q in range(MEMBERS)]
FACE = sum(1 for q in range(MEMBERS) if VELOCITY[q][0] == 1)
UP = [q for q in range(MEMBERS) if VELOCITY[q][1] == 1]
DOWN = [q for q in range(MEMBERS) if VELOCITY[q][1] == -1]
ROUNDS = 5
FORWARD_0, SEED, FORWARD_1, BACK_2, BACK_1 = range(ROUNDS)
MESH = pl.DeviceIdType.MESH


def flow_moments(f):
    s = {q: f[q] + f[q + 1] for q in range(1, 19, 2)}
    d = {q: f[q] - f[q + 1] for q in range(1, 19, 2)}
    xy, xz, yz = s[7] + s[9], s[11] + s[13], s[15] + s[17]
    total = (f[0] + s[1] + s[3]) + (s[5] + xy) + (xz + yz)
    first = (
        (d[1] + d[7]) + (d[9] + d[11]) + d[13],
        (d[3] + d[7]) + (d[15] - d[9]) + d[17],
        (d[5] + d[11]) + (d[15] - d[13]) - d[17],
    )
    second = (
        s[1] + (xy + xz), s[3] + (xy + yz), s[5] + (xz + yz),
        s[7] - s[9], s[11] - s[13], s[15] - s[17],
    )
    return total, first, second


def spread(even, vector, tensor):
    x, y, z = vector
    xx, yy, zz, xy, xz, yz = tensor
    out = [even]

    def pair(e, o):
        out.append(e + o)
        out.append(e - o)

    ex, ey, ez = even + xx, even + yy, even + zz
    pair(ex, x)
    pair(ey, y)
    pair(ez, z)
    for e, cross, first, second in (
        (ex + yy, xy + xy, x, y), (ex + zz, xz + xz, x, z), (ey + zz, yz + yz, y, z)
    ):
        pair(e + cross, first + second)
        pair(e - cross, first - second)
    return out


def dot(a, b):
    return (a[0] * b[0] + a[1] * b[1]) + a[2] * b[2]


def state_moments(f, g, slow):
    density, momentum, second = flow_moments(f)
    third = density * (1.0 / 3.0)
    stress = tuple(m - third for m in second[:3]) + second[3:]
    u = tuple(slow * m for m in momentum)
    heat = (g[0] + (g[1] + g[2])) + ((g[3] + g[4]) + (g[5] + g[6]))
    flux = (g[1] - g[2], g[3] - g[4], g[5] - g[6])
    ease = jnp.exp(-2.0 * (heat - 1.0))
    omega = 1.0 / (0.5 + 0.3 * ease)
    return density, u, stress, heat, flux, omega, ease


def collide(f, g, solid, kappa, moments):
    density, u, stress, heat, flux, omega, _ = moments
    k_u, k_s = 4.5 * omega, 4.5 * (1.2 - omega)
    ku = tuple(k_u * m for m in u)
    tensor = (
        ku[0] * u[0] + k_s * stress[0], ku[1] * u[1] + k_s * stress[1],
        ku[2] * u[2] + k_s * stress[2], ku[0] * u[1] + k_s * stress[3],
        ku[0] * u[2] + k_s * stress[4], ku[1] * u[2] + k_s * stress[5],
    )
    even = 1.2 * density - (tensor[0] + tensor[1] + tensor[2]) * (1.0 / 3.0)
    vector = tuple(3.6 * m for m in u)
    w = 1.0 / 36.0
    relaxed = spread(
        w * even, tuple(w * m for m in vector), tuple(w * m for m in tensor)
    )
    out = []
    for q in range(19):
        scale = 12.0 if q == 0 else 2.0 if q < 7 else 1.0
        fluid = (relaxed[q] if scale == 1.0 else scale * relaxed[q]) - GHOST * f[q]
        out.append(jnp.where(solid, f[OPPOSITE[q]], fluid))
    sigma, pull = 1.4 - kappa, kappa * heat
    gate = tuple(0.5 * (pull * a + sigma * b) for a, b in zip(u, flux))
    base = (1.4 / 8.0) * heat
    out.append(2.0 * base - HEAT_GHOST * g[0])
    for axis in range(3):
        a, b = g[1 + 2 * axis], g[2 + 2 * axis]
        out.append((base + gate[axis]) - HEAT_GHOST * a)
        out.append((base - gate[axis]) - HEAT_GHOST * b)
    return out


def adjoint_sums(l, m, fluid):
    weighted = [12.0 * l[0]] + [2.0 * v for v in l[1:7]] + list(l[7:19])
    even, vector, tensor = flow_moments(weighted)
    scale = fluid * (1.0 / 36.0)
    even = scale * even
    vector = tuple(scale * v for v in vector)
    third = even * (1.0 / 3.0)
    tensor = tuple(scale * v - third for v in tensor[:3]) + tuple(scale * v for v in tensor[3:])
    gate = tuple(0.5 * (m[1 + 2 * k] - m[2 + 2 * k]) for k in range(3))
    return even, vector, tensor, gate


def sensitivities(sums, u, heat, flux, omega, kappa):
    _, vector, (xx, yy, zz, xy, xz, yz), gate = sums
    bent = (
        (xx * u[0] + xy * u[1]) + xz * u[2],
        (xy * u[0] + yy * u[1]) + yz * u[2],
        (xz * u[0] + yz * u[1]) + zz * u[2],
    )
    k_u, pull = 9.0 * omega, kappa * heat
    back = tuple(k_u * b + (3.6 * v + pull * e) for b, v, e in zip(bent, vector, gate))
    resist = dot(u, back)
    conduct = dot(gate, tuple(heat * a - b for a, b in zip(u, flux)))
    return back, bent, resist, conduct


def collide_back(l, m, sums, moments, back, bent, solid, slow, kappa):
    even, vector, tensor, gate = sums
    _, u, stress, heat, flux, omega, ease = moments
    xx, yy, zz, xy, xz, yz = tensor
    cross = xy * stress[3] + xz * stress[4] + yz * stress[5]
    inner = (xx * stress[0] + yy * stress[1]) + (zz * stress[2] + (cross + cross))
    omega_back = 4.5 * (dot(u, bent) - inner)
    k_s = 4.5 * (1.2 - omega)
    stress_back = tuple(k_s * t for t in tensor)
    density_back = 1.2 * even - (stress_back[0] + stress_back[1] + stress_back[2]) * (1.0 / 3.0)
    momentum_back = tuple(slow * b for b in back)
    smooth = spread(density_back, momentum_back, stress_back)
    out = []
    for q in range(19):
        out.append(jnp.where(solid, l[OPPOSITE[q]], -GHOST * l[q]) + smooth[q])
    moved = (m[0] + m[0] + (m[1] + m[2])) + ((m[3] + m[4]) + (m[5] + m[6]))
    heat_back = (1.4 / 8.0) * moved + kappa * dot(gate, u) + omega_back * (0.6 * ease) * (omega * omega)
    sigma = 1.4 - kappa
    flux_back = tuple(sigma * e for e in gate)
    out.append(heat_back - HEAT_GHOST * m[0])
    for axis in range(3):
        a, b = m[1 + 2 * axis], m[2 + 2 * axis]
        out.append((heat_back + flux_back[axis]) - HEAT_GHOST * a)
        out.append((heat_back - flux_back[axis]) - HEAT_GHOST * b)
    return out


def kernel(
    gx, gy, *refs
):
    whole, (resist_out, conduct_out), inputs = refs[:7], refs[7:9], refs[9:16]
    flow_ref, heat_ref, resist_ref, conduct_ref, solid_ref, flow_w_ref, heat_w_ref = inputs
    ext, own_edge, edge, saved, fields, load_sem, send_sem, recv_sem = refs[16:]
    width, height, depth = resist_ref.shape
    sides = edge.shape[1]
    me_x, me_y = lax.axis_index("gx"), lax.axis_index("gy")
    right, left = lax.rem(me_x + 1, gx), lax.rem(me_x + gx - 1, gx)
    up, down = lax.rem(me_y + 1, gy), lax.rem(me_y + gy - 1, gy)
    columns = [(up, 0)] if sides == 1 else [(up, 0), (down, 1)]

    loads = [
        pltpu.make_async_copy(src, dst, load_sem.at[k])
        for k, (src, dst) in enumerate(zip(whole, inputs))
    ]
    for load in loads:
        load.start()

    barrier = pltpu.get_barrier_semaphore()
    partners = [(right, me_y), (left, me_y)]
    for y, _ in columns:
        partners += [(me_x, y), (right, y), (left, y)]
    for partner in partners:
        pl.semaphore_signal(barrier, inc=1, device_id=partner, device_id_type=MESH)

    lane = lax.broadcasted_iota(jnp.int32, (height, depth), 1)

    def plane(i):
        return lax.rem(me_x + 1 + i, 2)

    def copies(r, i):
        x = plane(i)
        upper = x == width - 1
        beside = jnp.where(upper, right, left)
        halo = jnp.where(upper, 0, width + 1)
        group = pl.ds(jnp.where(upper, 0, FACE), FACE)

        def remote(k, src, dst, device):
            return pltpu.make_async_remote_copy(
                src_ref=src, dst_ref=dst,
                send_sem=send_sem.at[r, i, k], recv_sem=recv_sem.at[r, i, k],
                device_id=device, device_id_type=MESH,
            )

        across = [remote(0, ext.at[r, x + 1, group], ext.at[r, halo, group], (beside, me_y))]
        within = []
        for y, side in columns:
            k = 1 + 2 * side
            across.append(remote(k, own_edge.at[r, x], edge.at[r, side, halo], (beside, y)))
            within.append(remote(k + 1, own_edge.at[r, x], edge.at[r, side, x + 1], (me_x, y)))
        return across, within

    def start(r, i):
        across, within = copies(r, i)
        for copy in across + within:
            copy.start()

    def leave(r, x, members):
        packed = None
        for q in range(MEMBERS):
            if members[q] is None:
                continue
            value = members[q]
            _, step_y, step_z = VELOCITY[q]
            if step_z:
                value = pltpu.roll(value, step_z % height, 0)
            if step_y:
                value = pltpu.roll(value, step_y % depth, 1)
            ext[r, x + 1, SLOT[q]] = value
            if step_y:
                place = UP.index(q) if step_y == 1 else DOWN.index(q)
                shift = place * step_y % depth
                where = place if step_y == 1 else depth - 1 - place
                turned = pltpu.roll(value, shift, 1) if shift else value
                packed = turned if packed is None else jnp.where(lane == where, turned, packed)
        own_edge[r, x] = packed

    def gather(r, x, q):
        step_x, step_y, _ = VELOCITY[q]
        value = ext[r, x + 1 - step_x, SLOT[q]]
        if step_y:
            side = 0 if step_y == 1 else sides - 1
            packed = edge[r, side, x + 1 - step_x]
            place = UP.index(q) if step_y == 1 else DOWN.index(q)
            shift = -place * step_y % depth
            turned = pltpu.roll(packed, shift, 1) if shift else packed
            value = jnp.where(lane == (0 if step_y == 1 else depth - 1), turned, value)
        return value

    def keep(t, x, moments):
        _, u, stress, heat, flux, omega, ease = moments
        for k, value in enumerate((*u, heat, *flux, omega, ease, *stress)):
            saved[t, x, k] = value

    def kept(t, x, whole):
        values = [saved[t, x, k] for k in range(15 if whole else 8)]
        return (
            None, tuple(values[:3]), tuple(values[9:15]) if whole else None, values[3],
            tuple(values[4:7]), values[7], values[8] if whole else None,
        )

    def planes(body, after=(), then=None, early=None):
        for r in after:
            for i in range(2):
                for copy in copies(r, i)[1]:
                    copy.wait_recv()

        def step(i, carry):
            for r in after:
                for copy in copies(r, i)[0]:
                    copy.wait_recv()
            if early is not None:
                start(early, i)
            body(plane(i))
            if then is not None:
                start(then, i)
            return carry

        lax.fori_loop(0, 2, step, 0)

    def first(x):
        solid = solid_ref[x] != 0
        slow = jnp.where(solid, 0.0, 1.0) / (1.0 + resist_ref[x])
        kappa = 1.0 / (0.5 + 0.4 * conduct_ref[x])
        fields[x, 0] = slow
        fields[x, 1] = kappa
        f = [flow_ref[q, x] for q in range(19)]
        g = [heat_ref[q, x] for q in range(7)]
        moments = state_moments(f, g, slow)
        keep(0, x, moments)
        leave(FORWARD_0, x, collide(f, g, solid, kappa, moments))

    for load in loads[:5]:
        load.wait()
    planes(first)
    pl.semaphore_wait(barrier, len(partners))
    start(FORWARD_0, 1)
    start(FORWARD_0, 0)

    def seed(x):
        weights = [flow_w_ref[k, x] for k in range(3)]
        heat = heat_w_ref[x]
        members = [None] * MEMBERS
        for q in range(MEMBERS):
            if q >= 19:
                members[OPPOSITE[q]] = heat
            elif q:
                value = None
                for weight, step in zip(weights, VELOCITY[q]):
                    if step:
                        term = weight if step == 1 else -weight
                        value = term if value is None else value + term
                members[OPPOSITE[q]] = value
        leave(SEED, x, members)

    for load in loads[5:]:
        load.wait()
    planes(seed)

    def second(x):
        solid, slow, kappa = solid_ref[x] != 0, fields[x, 0], fields[x, 1]
        state = [gather(FORWARD_0, x, q) for q in range(MEMBERS)]
        f, g = state[:19], state[19:]
        moments = state_moments(f, g, slow)
        keep(1, x, moments)
        leave(FORWARD_1, x, collide(f, g, solid, kappa, moments))

    planes(second, after=(FORWARD_0,), then=FORWARD_1, early=SEED)

    def reverse(r, x, moments, target):
        solid, slow, kappa = solid_ref[x] != 0, fields[x, 0], fields[x, 1]
        back = [
            jnp.zeros((height, depth), jnp.float32) if r == SEED and q == 0
            else gather(r, x, OPPOSITE[q])
            for q in range(MEMBERS)
        ]
        l, m = back[:19], back[19:]
        sums = adjoint_sums(l, m, jnp.where(solid, 0.0, 1.0))
        _, u, _, heat, flux, omega, _ = moments
        u_back, bent, resist, conduct = sensitivities(sums, u, heat, flux, omega, kappa)
        if r == SEED:
            resist_out[x] = resist
            conduct_out[x] = conduct
        elif target is not None:
            resist_out[x] += resist
            conduct_out[x] += conduct
        else:
            resist_out[x] = -(resist_out[x] + resist) / (1.0 + resist_ref[x])
            conduct_out[x] = (conduct_out[x] + conduct) * (-0.4 * kappa * kappa)
        if target is not None:
            out = collide_back(l, m, sums, moments, u_back, bent, solid, slow, kappa)
            leave(target, x, [out[OPPOSITE[q]] for q in range(MEMBERS)])

    def third(x):
        state = [gather(FORWARD_1, x, q) for q in range(MEMBERS)]
        reverse(SEED, x, state_moments(state[:19], state[19:], fields[x, 0]), BACK_2)

    planes(third, after=(SEED, FORWARD_1), then=BACK_2)
    planes(
        lambda x: reverse(BACK_2, x, kept(1, x, True), BACK_1), after=(BACK_2,), then=BACK_1
    )
    planes(lambda x: reverse(BACK_1, x, kept(0, x, False), None), after=(BACK_1,))

    for r in range(ROUNDS):
        for i in range(2):
            across, within = copies(r, i)
            for copy in across + within:
                copy.wait_send()


def on_device(gx, gy, flow, heat, flow_weight, heat_weight, resistance, conductivity, solid_mask):
    shape = resistance.shape
    width, height, depth = shape
    sides = 1 if gy == 2 else 2
    count = 1 + 2 * sides
    args = (flow, heat, resistance, conductivity, solid_mask, flow_weight, heat_weight)
    far = pl.BlockSpec(memory_space=pltpu.HBM)
    near = pl.BlockSpec(memory_space=pltpu.VMEM)
    result = [jax.ShapeDtypeStruct(shape, jnp.float32)] * 2
    return pl.pallas_call(
        functools.partial(kernel, gx, gy),
        out_shape=result,
        in_specs=[far] * len(args),
        out_specs=[near] * 2,
        scratch_shapes=[pltpu.VMEM(a.shape, a.dtype) for a in args] + [
            pltpu.VMEM((ROUNDS, width + 2, MEMBERS, height, depth), jnp.float32),
            pltpu.VMEM((ROUNDS, width, height, depth), jnp.float32),
            pltpu.VMEM((ROUNDS, sides, width + 2, height, depth), jnp.float32),
            pltpu.VMEM((STEPS - 1, width, 15, height, depth), jnp.float32),
            pltpu.VMEM((width, 2, height, depth), jnp.float32),
            pltpu.SemaphoreType.DMA((len(args),)),
            pltpu.SemaphoreType.DMA((ROUNDS, 2, count)),
            pltpu.SemaphoreType.DMA((ROUNDS, 2, count)),
        ],
        compiler_params=pltpu.CompilerParams(
            collective_id=0, has_side_effects=True, vmem_limit_bytes=64 * 1024 * 1024
        ),
    )(*args)


def solution(mesh):
    wide, flat = P(None, "gx", None, "gy"), P("gx", None, "gy")
    return jax.shard_map(
        functools.partial(on_device, mesh.shape["gx"], mesh.shape["gy"]),
        mesh=mesh,
        in_specs=(wide, wide, wide, flat, flat, flat, flat),
        out_specs=(flat, flat),
        check_vma=False,
    )
```

```python
import functools

import jax
import jax.numpy as jnp
from jax import lax
from jax.experimental import pallas as pl
from jax.experimental.pallas import tpu as pltpu
from jax.sharding import PartitionSpec as P

STEPS = 3
GHOST = 0.2
HEAT_GHOST = 0.4

FLOW = [
    (0, 0, 0), (1, 0, 0), (-1, 0, 0), (0, 1, 0), (0, -1, 0), (0, 0, 1), (0, 0, -1),
    (1, 1, 0), (-1, -1, 0), (1, -1, 0), (-1, 1, 0), (1, 0, 1), (-1, 0, -1),
    (1, 0, -1), (-1, 0, 1), (0, 1, 1), (0, -1, -1), (0, 1, -1), (0, -1, 1),
]
VELOCITY = FLOW + FLOW[:7]
MEMBERS = len(VELOCITY)
OPPOSITE = [0] + [q + 1 if q % 2 else q - 1 for q in range(1, 19)]
OPPOSITE = OPPOSITE + [19 + q for q in OPPOSITE[:7]]
ORDER = (
    [q for q in range(MEMBERS) if VELOCITY[q][0] == 1]
    + [q for q in range(MEMBERS) if VELOCITY[q][0] == -1]
    + [q for q in range(MEMBERS) if VELOCITY[q][0] == 0]
)
SLOT = [ORDER.index(q) for q in range(MEMBERS)]
FACE = sum(1 for q in range(MEMBERS) if VELOCITY[q][0] == 1)
UP = [q for q in range(MEMBERS) if VELOCITY[q][1] == 1]
DOWN = [q for q in range(MEMBERS) if VELOCITY[q][1] == -1]
ROUNDS = 5
FORWARD_0, SEED, FORWARD_1, BACK_2, BACK_1 = range(ROUNDS)
MESH = pl.DeviceIdType.MESH


def flow_moments(f):
    s = {q: f[q] + f[q + 1] for q in range(1, 19, 2)}
    d = {q: f[q] - f[q + 1] for q in range(1, 19, 2)}
    xy, xz, yz = s[7] + s[9], s[11] + s[13], s[15] + s[17]
    total = (f[0] + s[1] + s[3]) + (s[5] + xy) + (xz + yz)
    first = (
        (d[1] + d[7]) + (d[9] + d[11]) + d[13],
        (d[3] + d[7]) + (d[15] - d[9]) + d[17],
        (d[5] + d[11]) + (d[15] - d[13]) - d[17],
    )
    second = (
        s[1] + (xy + xz), s[3] + (xy + yz), s[5] + (xz + yz),
        s[7] - s[9], s[11] - s[13], s[15] - s[17],
    )
    return total, first, second


def spread(even, vector, tensor):
    x, y, z = vector
    xx, yy, zz, xy, xz, yz = tensor
    out = [even]

    def pair(e, o):
        out.append(e + o)
        out.append(e - o)

    ex, ey, ez = even + xx, even + yy, even + zz
    pair(ex, x)
    pair(ey, y)
    pair(ez, z)
    for e, cross, first, second in (
        (ex + yy, xy + xy, x, y), (ex + zz, xz + xz, x, z), (ey + zz, yz + yz, y, z)
    ):
        pair(e + cross, first + second)
        pair(e - cross, first - second)
    return out


def dot(a, b):
    return (a[0] * b[0] + a[1] * b[1]) + a[2] * b[2]


def state_moments(f, g, slow):
    density, momentum, second = flow_moments(f)
    third = density * (1.0 / 3.0)
    stress = tuple(m - third for m in second[:3]) + second[3:]
    u = tuple(slow * m for m in momentum)
    heat = (g[0] + (g[1] + g[2])) + ((g[3] + g[4]) + (g[5] + g[6]))
    flux = (g[1] - g[2], g[3] - g[4], g[5] - g[6])
    ease = jnp.exp(-2.0 * (heat - 1.0))
    omega = 1.0 / (0.5 + 0.3 * ease)
    return density, u, stress, heat, flux, omega, ease


def collide(f, g, solid, kappa, moments):
    density, u, stress, heat, flux, omega, _ = moments
    k_u, k_s = 4.5 * omega, 4.5 * (1.2 - omega)
    ku = tuple(k_u * m for m in u)
    tensor = (
        ku[0] * u[0] + k_s * stress[0], ku[1] * u[1] + k_s * stress[1],
        ku[2] * u[2] + k_s * stress[2], ku[0] * u[1] + k_s * stress[3],
        ku[0] * u[2] + k_s * stress[4], ku[1] * u[2] + k_s * stress[5],
    )
    even = 1.2 * density - (tensor[0] + tensor[1] + tensor[2]) * (1.0 / 3.0)
    vector = tuple(3.6 * m for m in u)
    w = 1.0 / 36.0
    relaxed = spread(
        w * even, tuple(w * m for m in vector), tuple(w * m for m in tensor)
    )
    out = []
    for q in range(19):
        scale = 12.0 if q == 0 else 2.0 if q < 7 else 1.0
        fluid = (relaxed[q] if scale == 1.0 else scale * relaxed[q]) - GHOST * f[q]
        out.append(jnp.where(solid, f[OPPOSITE[q]], fluid))
    sigma, pull = 1.4 - kappa, kappa * heat
    gate = tuple(0.5 * (pull * a + sigma * b) for a, b in zip(u, flux))
    base = (1.4 / 8.0) * heat
    out.append(2.0 * base - HEAT_GHOST * g[0])
    for axis in range(3):
        a, b = g[1 + 2 * axis], g[2 + 2 * axis]
        out.append((base + gate[axis]) - HEAT_GHOST * a)
        out.append((base - gate[axis]) - HEAT_GHOST * b)
    return out


def adjoint_sums(l, m, fluid):
    weighted = [12.0 * l[0]] + [2.0 * v for v in l[1:7]] + list(l[7:19])
    even, vector, tensor = flow_moments(weighted)
    scale = fluid * (1.0 / 36.0)
    even = scale * even
    vector = tuple(scale * v for v in vector)
    third = even * (1.0 / 3.0)
    tensor = tuple(scale * v - third for v in tensor[:3]) + tuple(scale * v for v in tensor[3:])
    gate = tuple(0.5 * (m[1 + 2 * k] - m[2 + 2 * k]) for k in range(3))
    return even, vector, tensor, gate


def sensitivities(sums, u, heat, flux, omega, kappa):
    _, vector, (xx, yy, zz, xy, xz, yz), gate = sums
    bent = (
        (xx * u[0] + xy * u[1]) + xz * u[2],
        (xy * u[0] + yy * u[1]) + yz * u[2],
        (xz * u[0] + yz * u[1]) + zz * u[2],
    )
    k_u, pull = 9.0 * omega, kappa * heat
    back = tuple(k_u * b + (3.6 * v + pull * e) for b, v, e in zip(bent, vector, gate))
    resist = dot(u, back)
    conduct = dot(gate, tuple(heat * a - b for a, b in zip(u, flux)))
    return back, bent, resist, conduct


def collide_back(l, m, sums, moments, back, bent, solid, slow, kappa):
    even, vector, tensor, gate = sums
    _, u, stress, heat, flux, omega, ease = moments
    xx, yy, zz, xy, xz, yz = tensor
    cross = xy * stress[3] + xz * stress[4] + yz * stress[5]
    inner = (xx * stress[0] + yy * stress[1]) + (zz * stress[2] + (cross + cross))
    omega_back = 4.5 * (dot(u, bent) - inner)
    k_s = 4.5 * (1.2 - omega)
    stress_back = tuple(k_s * t for t in tensor)
    density_back = 1.2 * even - (stress_back[0] + stress_back[1] + stress_back[2]) * (1.0 / 3.0)
    momentum_back = tuple(slow * b for b in back)
    smooth = spread(density_back, momentum_back, stress_back)
    out = []
    for q in range(19):
        out.append(jnp.where(solid, l[OPPOSITE[q]], -GHOST * l[q]) + smooth[q])
    moved = (m[0] + m[0] + (m[1] + m[2])) + ((m[3] + m[4]) + (m[5] + m[6]))
    heat_back = (1.4 / 8.0) * moved + kappa * dot(gate, u) + omega_back * (0.6 * ease) * (omega * omega)
    sigma = 1.4 - kappa
    flux_back = tuple(sigma * e for e in gate)
    out.append(heat_back - HEAT_GHOST * m[0])
    for axis in range(3):
        a, b = m[1 + 2 * axis], m[2 + 2 * axis]
        out.append((heat_back + flux_back[axis]) - HEAT_GHOST * a)
        out.append((heat_back - flux_back[axis]) - HEAT_GHOST * b)
    return out


def kernel(
    gx, gy, *refs
):
    whole, result, inputs = refs[:7], refs[7], refs[8:15]
    resist_out, conduct_out = result.at[0], result.at[1]
    flow_ref, heat_ref, resist_ref, conduct_ref, solid_ref, flow_w_ref, heat_w_ref = inputs
    ext, own_edge, edge, saved, fields, load_sem, send_sem, recv_sem = refs[15:]
    width, height, depth = resist_ref.shape
    sides = edge.shape[1]
    me_x, me_y = lax.axis_index("gx"), lax.axis_index("gy")
    right, left = lax.rem(me_x + 1, gx), lax.rem(me_x + gx - 1, gx)
    up, down = lax.rem(me_y + 1, gy), lax.rem(me_y + gy - 1, gy)
    columns = [(up, 0)] if sides == 1 else [(up, 0), (down, 1)]

    loads = [
        pltpu.make_async_copy(src, dst, load_sem.at[k])
        for k, (src, dst) in enumerate(zip(whole, inputs))
    ]
    for load in loads:
        load.start()

    barrier = pltpu.get_barrier_semaphore()
    partners = [(right, me_y), (left, me_y)]
    for y, _ in columns:
        partners += [(me_x, y), (right, y), (left, y)]
    for partner in partners:
        pl.semaphore_signal(barrier, inc=1, device_id=partner, device_id_type=MESH)

    lane = lax.broadcasted_iota(jnp.int32, (height, depth), 1)

    def plane(i):
        return lax.rem(me_x + 1 + i, 2)

    def copies(r, i):
        x = plane(i)
        upper = x == width - 1
        beside = jnp.where(upper, right, left)
        halo = jnp.where(upper, 0, width + 1)
        group = pl.ds(jnp.where(upper, 0, FACE), FACE)

        def remote(k, src, dst, device):
            return pltpu.make_async_remote_copy(
                src_ref=src, dst_ref=dst,
                send_sem=send_sem.at[r, i, k], recv_sem=recv_sem.at[r, i, k],
                device_id=device, device_id_type=MESH,
            )

        across = [remote(0, ext.at[r, x + 1, group], ext.at[r, halo, group], (beside, me_y))]
        within = []
        for y, side in columns:
            k = 1 + 2 * side
            across.append(remote(k, own_edge.at[r, x], edge.at[r, side, halo], (beside, y)))
            within.append(remote(k + 1, own_edge.at[r, x], edge.at[r, side, x + 1], (me_x, y)))
        return across, within

    def start(r, i):
        across, within = copies(r, i)
        for copy in across + within:
            copy.start()

    def leave(r, x, members):
        packed = None
        for q in range(MEMBERS):
            if members[q] is None:
                continue
            value = members[q]
            _, step_y, step_z = VELOCITY[q]
            if step_z:
                value = pltpu.roll(value, step_z % height, 0)
            if step_y:
                value = pltpu.roll(value, step_y % depth, 1)
            ext[r, x + 1, SLOT[q]] = value
            if step_y:
                place = UP.index(q) if step_y == 1 else DOWN.index(q)
                shift = place * step_y % depth
                where = place if step_y == 1 else depth - 1 - place
                turned = pltpu.roll(value, shift, 1) if shift else value
                packed = turned if packed is None else jnp.where(lane == where, turned, packed)
        own_edge[r, x] = packed

    def gather(r, x, q):
        step_x, step_y, _ = VELOCITY[q]
        value = ext[r, x + 1 - step_x, SLOT[q]]
        if step_y:
            side = 0 if step_y == 1 else sides - 1
            packed = edge[r, side, x + 1 - step_x]
            place = UP.index(q) if step_y == 1 else DOWN.index(q)
            shift = -place * step_y % depth
            turned = pltpu.roll(packed, shift, 1) if shift else packed
            value = jnp.where(lane == (0 if step_y == 1 else depth - 1), turned, value)
        return value

    def keep(t, x, moments):
        _, u, stress, heat, flux, omega, ease = moments
        for k, value in enumerate((*u, heat, *flux, omega, ease, *stress)):
            saved[t, x, k] = value

    def kept(t, x, whole):
        values = [saved[t, x, k] for k in range(15 if whole else 8)]
        return (
            None, tuple(values[:3]), tuple(values[9:15]) if whole else None, values[3],
            tuple(values[4:7]), values[7], values[8] if whole else None,
        )

    def planes(body, after=(), then=None, early=None):
        for r in after:
            for i in range(2):
                for copy in copies(r, i)[1]:
                    copy.wait_recv()

        if early is not None:
            start(early, 1)
            start(early, 0)

        def step(i, carry):
            for r in after:
                for copy in copies(r, i)[0]:
                    copy.wait_recv()
            body(plane(i))
            if then is not None:
                start(then, i)
            return carry

        lax.fori_loop(0, 2, step, 0)

    def first(x):
        solid = solid_ref[x] != 0
        slow = jnp.where(solid, 0.0, 1.0) / (1.0 + resist_ref[x])
        kappa = 1.0 / (0.5 + 0.4 * conduct_ref[x])
        fields[x, 0] = slow
        fields[x, 1] = kappa
        f = [flow_ref[q, x] for q in range(19)]
        g = [heat_ref[q, x] for q in range(7)]
        moments = state_moments(f, g, slow)
        keep(0, x, moments)
        leave(FORWARD_0, x, collide(f, g, solid, kappa, moments))

    for load in loads[:5]:
        load.wait()
    planes(first)
    pl.semaphore_wait(barrier, len(partners))
    start(FORWARD_0, 1)
    start(FORWARD_0, 0)

    def seed(x):
        weights = [flow_w_ref[k, x] for k in range(3)]
        heat = heat_w_ref[x]
        members = [None] * MEMBERS
        for q in range(MEMBERS):
            if q >= 19:
                members[OPPOSITE[q]] = heat
            elif q:
                value = None
                for weight, step in zip(weights, VELOCITY[q]):
                    if step:
                        term = weight if step == 1 else -weight
                        value = term if value is None else value + term
                members[OPPOSITE[q]] = value
        leave(SEED, x, members)

    for load in loads[5:]:
        load.wait()
    planes(seed)

    def second(x):
        solid, slow, kappa = solid_ref[x] != 0, fields[x, 0], fields[x, 1]
        state = [gather(FORWARD_0, x, q) for q in range(MEMBERS)]
        f, g = state[:19], state[19:]
        moments = state_moments(f, g, slow)
        keep(1, x, moments)
        leave(FORWARD_1, x, collide(f, g, solid, kappa, moments))

    planes(second, after=(FORWARD_0,), then=FORWARD_1, early=SEED)

    def reverse(r, x, moments, target):
        solid, slow, kappa = solid_ref[x] != 0, fields[x, 0], fields[x, 1]
        back = [
            jnp.zeros((height, depth), jnp.float32) if r == SEED and q == 0
            else gather(r, x, OPPOSITE[q])
            for q in range(MEMBERS)
        ]
        l, m = back[:19], back[19:]
        sums = adjoint_sums(l, m, jnp.where(solid, 0.0, 1.0))
        _, u, _, heat, flux, omega, _ = moments
        u_back, bent, resist, conduct = sensitivities(sums, u, heat, flux, omega, kappa)
        if r == SEED:
            resist_out[x] = resist
            conduct_out[x] = conduct
        elif target is not None:
            resist_out[x] += resist
            conduct_out[x] += conduct
        else:
            resist_out[x] = -(resist_out[x] + resist) / (1.0 + resist_ref[x])
            conduct_out[x] = (conduct_out[x] + conduct) * (-0.4 * kappa * kappa)
        if target is not None:
            out = collide_back(l, m, sums, moments, u_back, bent, solid, slow, kappa)
            leave(target, x, [out[OPPOSITE[q]] for q in range(MEMBERS)])

    def third(x):
        state = [gather(FORWARD_1, x, q) for q in range(MEMBERS)]
        reverse(SEED, x, state_moments(state[:19], state[19:], fields[x, 0]), BACK_2)

    planes(third, after=(SEED, FORWARD_1), then=BACK_2)
    planes(
        lambda x: reverse(BACK_2, x, kept(1, x, True), BACK_1), after=(BACK_2,), then=BACK_1
    )
    planes(lambda x: reverse(BACK_1, x, kept(0, x, False), None), after=(BACK_1,))

    for r in range(ROUNDS):
        for i in range(2):
            across, within = copies(r, i)
            for copy in across + within:
                copy.wait_send()


def on_device(gx, gy, flow, heat, flow_weight, heat_weight, resistance, conductivity, solid_mask):
    shape = resistance.shape
    width, height, depth = shape
    sides = 1 if gy == 2 else 2
    count = 1 + 2 * sides
    args = (flow, heat, resistance, conductivity, solid_mask, flow_weight, heat_weight)
    far = pl.BlockSpec(memory_space=pltpu.HBM)
    near = pl.BlockSpec(memory_space=pltpu.VMEM)
    found = pl.pallas_call(
        functools.partial(kernel, gx, gy),
        out_shape=jax.ShapeDtypeStruct((2,) + shape, jnp.float32),
        in_specs=[far] * len(args),
        out_specs=near,
        scratch_shapes=[pltpu.VMEM(a.shape, a.dtype) for a in args] + [
            pltpu.VMEM((ROUNDS, width + 2, MEMBERS, height, depth), jnp.float32),
            pltpu.VMEM((ROUNDS, width, height, depth), jnp.float32),
            pltpu.VMEM((ROUNDS, sides, width + 2, height, depth), jnp.float32),
            pltpu.VMEM((STEPS - 1, width, 15, height, depth), jnp.float32),
            pltpu.VMEM((width, 2, height, depth), jnp.float32),
            pltpu.SemaphoreType.DMA((len(args),)),
            pltpu.SemaphoreType.DMA((ROUNDS, 2, count)),
            pltpu.SemaphoreType.DMA((ROUNDS, 2, count)),
        ],
        compiler_params=pltpu.CompilerParams(
            collective_id=0, has_side_effects=True, vmem_limit_bytes=64 * 1024 * 1024
        ),
    )(*args)
    return found[0], found[1]


def solution(mesh):
    wide, flat = P(None, "gx", None, "gy"), P("gx", None, "gy")
    return jax.shard_map(
        functools.partial(on_device, mesh.shape["gx"], mesh.shape["gy"]),
        mesh=mesh,
        in_specs=(wide, wide, wide, flat, flat, flat, flat),
        out_specs=(flat, flat),
        check_vma=False,
    )
```

```python
import functools

import jax
import jax.numpy as jnp
from jax import lax
from jax.experimental import pallas as pl
from jax.experimental.pallas import tpu as pltpu
from jax.sharding import PartitionSpec as P

STEPS = 3
GHOST = 0.2
HEAT_GHOST = 0.4

FLOW = [
    (0, 0, 0), (1, 0, 0), (-1, 0, 0), (0, 1, 0), (0, -1, 0), (0, 0, 1), (0, 0, -1),
    (1, 1, 0), (-1, -1, 0), (1, -1, 0), (-1, 1, 0), (1, 0, 1), (-1, 0, -1),
    (1, 0, -1), (-1, 0, 1), (0, 1, 1), (0, -1, -1), (0, 1, -1), (0, -1, 1),
]
VELOCITY = FLOW + FLOW[:7]
MEMBERS = len(VELOCITY)
OPPOSITE = [0] + [q + 1 if q % 2 else q - 1 for q in range(1, 19)]
OPPOSITE = OPPOSITE + [19 + q for q in OPPOSITE[:7]]
ORDER = (
    [q for q in range(MEMBERS) if VELOCITY[q][0] == 1]
    + [q for q in range(MEMBERS) if VELOCITY[q][0] == -1]
    + [q for q in range(MEMBERS) if VELOCITY[q][0] == 0]
)
SLOT = [ORDER.index(q) for q in range(MEMBERS)]
FACE = sum(1 for q in range(MEMBERS) if VELOCITY[q][0] == 1)
UP = [q for q in range(MEMBERS) if VELOCITY[q][1] == 1]
DOWN = [q for q in range(MEMBERS) if VELOCITY[q][1] == -1]
ROUNDS = 5
FORWARD_0, SEED, FORWARD_1, BACK_2, BACK_1 = range(ROUNDS)
MESH = pl.DeviceIdType.MESH


def flow_moments(f):
    s = {q: f[q] + f[q + 1] for q in range(1, 19, 2)}
    d = {q: f[q] - f[q + 1] for q in range(1, 19, 2)}
    xy, xz, yz = s[7] + s[9], s[11] + s[13], s[15] + s[17]
    total = (f[0] + s[1] + s[3]) + (s[5] + xy) + (xz + yz)
    first = (
        (d[1] + d[7]) + (d[9] + d[11]) + d[13],
        (d[3] + d[7]) + (d[15] - d[9]) + d[17],
        (d[5] + d[11]) + (d[15] - d[13]) - d[17],
    )
    second = (
        s[1] + (xy + xz), s[3] + (xy + yz), s[5] + (xz + yz),
        s[7] - s[9], s[11] - s[13], s[15] - s[17],
    )
    return total, first, second


def spread(even, vector, tensor):
    x, y, z = vector
    xx, yy, zz, xy, xz, yz = tensor
    out = [even]

    def pair(e, o):
        out.append(e + o)
        out.append(e - o)

    ex, ey, ez = even + xx, even + yy, even + zz
    pair(ex, x)
    pair(ey, y)
    pair(ez, z)
    for e, cross, first, second in (
        (ex + yy, xy + xy, x, y), (ex + zz, xz + xz, x, z), (ey + zz, yz + yz, y, z)
    ):
        pair(e + cross, first + second)
        pair(e - cross, first - second)
    return out


def dot(a, b):
    return (a[0] * b[0] + a[1] * b[1]) + a[2] * b[2]


def state_moments(f, g, slow):
    density, momentum, second = flow_moments(f)
    third = density * (1.0 / 3.0)
    stress = tuple(m - third for m in second[:3]) + second[3:]
    u = tuple(slow * m for m in momentum)
    heat = (g[0] + (g[1] + g[2])) + ((g[3] + g[4]) + (g[5] + g[6]))
    flux = (g[1] - g[2], g[3] - g[4], g[5] - g[6])
    ease = jnp.exp(-2.0 * (heat - 1.0))
    omega = 1.0 / (0.5 + 0.3 * ease)
    return density, u, stress, heat, flux, omega, ease


def collide(f, g, solid, kappa, moments):
    density, u, stress, heat, flux, omega, _ = moments
    k_u, k_s = 4.5 * omega, 4.5 * (1.2 - omega)
    ku = tuple(k_u * m for m in u)
    tensor = (
        ku[0] * u[0] + k_s * stress[0], ku[1] * u[1] + k_s * stress[1],
        ku[2] * u[2] + k_s * stress[2], ku[0] * u[1] + k_s * stress[3],
        ku[0] * u[2] + k_s * stress[4], ku[1] * u[2] + k_s * stress[5],
    )
    even = 1.2 * density - (tensor[0] + tensor[1] + tensor[2]) * (1.0 / 3.0)
    vector = tuple(3.6 * m for m in u)
    w = 1.0 / 36.0
    relaxed = spread(
        w * even, tuple(w * m for m in vector), tuple(w * m for m in tensor)
    )
    out = []
    for q in range(19):
        scale = 12.0 if q == 0 else 2.0 if q < 7 else 1.0
        fluid = (relaxed[q] if scale == 1.0 else scale * relaxed[q]) - GHOST * f[q]
        out.append(jnp.where(solid, f[OPPOSITE[q]], fluid))
    sigma, pull = 1.4 - kappa, kappa * heat
    gate = tuple(0.5 * (pull * a + sigma * b) for a, b in zip(u, flux))
    base = (1.4 / 8.0) * heat
    out.append(2.0 * base - HEAT_GHOST * g[0])
    for axis in range(3):
        a, b = g[1 + 2 * axis], g[2 + 2 * axis]
        out.append((base + gate[axis]) - HEAT_GHOST * a)
        out.append((base - gate[axis]) - HEAT_GHOST * b)
    return out


def adjoint_sums(l, m, fluid):
    weighted = [12.0 * l[0]] + [2.0 * v for v in l[1:7]] + list(l[7:19])
    even, vector, tensor = flow_moments(weighted)
    scale = fluid * (1.0 / 36.0)
    even = scale * even
    vector = tuple(scale * v for v in vector)
    third = even * (1.0 / 3.0)
    tensor = tuple(scale * v - third for v in tensor[:3]) + tuple(scale * v for v in tensor[3:])
    gate = tuple(0.5 * (m[1 + 2 * k] - m[2 + 2 * k]) for k in range(3))
    return even, vector, tensor, gate


def sensitivities(sums, u, heat, flux, omega, kappa):
    _, vector, (xx, yy, zz, xy, xz, yz), gate = sums
    bent = (
        (xx * u[0] + xy * u[1]) + xz * u[2],
        (xy * u[0] + yy * u[1]) + yz * u[2],
        (xz * u[0] + yz * u[1]) + zz * u[2],
    )
    k_u, pull = 9.0 * omega, kappa * heat
    back = tuple(k_u * b + (3.6 * v + pull * e) for b, v, e in zip(bent, vector, gate))
    resist = dot(u, back)
    conduct = dot(gate, tuple(heat * a - b for a, b in zip(u, flux)))
    return back, bent, resist, conduct


def collide_back(l, m, sums, moments, back, bent, solid, slow, kappa):
    even, vector, tensor, gate = sums
    _, u, stress, heat, flux, omega, ease = moments
    xx, yy, zz, xy, xz, yz = tensor
    cross = xy * stress[3] + xz * stress[4] + yz * stress[5]
    inner = (xx * stress[0] + yy * stress[1]) + (zz * stress[2] + (cross + cross))
    omega_back = 4.5 * (dot(u, bent) - inner)
    k_s = 4.5 * (1.2 - omega)
    stress_back = tuple(k_s * t for t in tensor)
    density_back = 1.2 * even - (stress_back[0] + stress_back[1] + stress_back[2]) * (1.0 / 3.0)
    momentum_back = tuple(slow * b for b in back)
    smooth = spread(density_back, momentum_back, stress_back)
    out = []
    for q in range(19):
        out.append(jnp.where(solid, l[OPPOSITE[q]], -GHOST * l[q]) + smooth[q])
    moved = (m[0] + m[0] + (m[1] + m[2])) + ((m[3] + m[4]) + (m[5] + m[6]))
    heat_back = (1.4 / 8.0) * moved + kappa * dot(gate, u) + omega_back * (0.6 * ease) * (omega * omega)
    sigma = 1.4 - kappa
    flux_back = tuple(sigma * e for e in gate)
    out.append(heat_back - HEAT_GHOST * m[0])
    for axis in range(3):
        a, b = m[1 + 2 * axis], m[2 + 2 * axis]
        out.append((heat_back + flux_back[axis]) - HEAT_GHOST * a)
        out.append((heat_back - flux_back[axis]) - HEAT_GHOST * b)
    return out


def kernel(
    gx, gy, *refs
):
    whole, result, inputs = refs[:7], refs[7], refs[8:15]
    resist_out, conduct_out = result.at[0], result.at[1]
    flow_ref, heat_ref, resist_ref, conduct_ref, solid_ref, flow_w_ref, heat_w_ref = inputs
    ext, own_edge, edge, saved, fields, load_sem, send_sem, recv_sem = refs[15:]
    width, height, depth = resist_ref.shape
    sides = edge.shape[1]
    me_x, me_y = lax.axis_index("gx"), lax.axis_index("gy")
    right, left = lax.rem(me_x + 1, gx), lax.rem(me_x + gx - 1, gx)
    up, down = lax.rem(me_y + 1, gy), lax.rem(me_y + gy - 1, gy)
    columns = [(up, 0)] if sides == 1 else [(up, 0), (down, 1)]

    loads = [
        pltpu.make_async_copy(src, dst, load_sem.at[k])
        for k, (src, dst) in enumerate(zip(whole, inputs))
    ]
    for load in loads:
        load.start()

    barrier = pltpu.get_barrier_semaphore()
    partners = [(right, me_y), (left, me_y)]
    for y, _ in columns:
        partners += [(me_x, y), (right, y), (left, y)]
    for partner in partners:
        pl.semaphore_signal(barrier, inc=1, device_id=partner, device_id_type=MESH)

    lane = lax.broadcasted_iota(jnp.int32, (height, depth), 1)

    def plane(i):
        return lax.rem(me_x + 1 + i, 2)

    def copies(r, i):
        x = plane(i)
        upper = x == width - 1
        beside = jnp.where(upper, right, left)
        halo = jnp.where(upper, 0, width + 1)
        group = pl.ds(jnp.where(upper, 0, FACE), FACE)

        def remote(k, src, dst, device):
            return pltpu.make_async_remote_copy(
                src_ref=src, dst_ref=dst,
                send_sem=send_sem.at[r, i, k], recv_sem=recv_sem.at[r, i, k],
                device_id=device, device_id_type=MESH,
            )

        across, within = [], []
        for y, side in columns:
            k = 1 + 2 * side
            across.append(remote(k, own_edge.at[r, x], edge.at[r, side, halo], (beside, y)))
            within.append(remote(k + 1, own_edge.at[r, x], edge.at[r, side, x + 1], (me_x, y)))
        across.append(
            remote(0, ext.at[r, x + 1, group], ext.at[r, halo, group], (beside, me_y))
        )
        return across, within

    def start(r, i):
        across, within = copies(r, i)
        for copy in across + within:
            copy.start()

    def leave(r, x, members):
        packed = None
        for q in range(MEMBERS):
            if members[q] is None:
                continue
            value = members[q]
            _, step_y, step_z = VELOCITY[q]
            if step_z:
                value = pltpu.roll(value, step_z % height, 0)
            if step_y:
                value = pltpu.roll(value, step_y % depth, 1)
            ext[r, x + 1, SLOT[q]] = value
            if step_y:
                place = UP.index(q) if step_y == 1 else DOWN.index(q)
                shift = place * step_y % depth
                where = place if step_y == 1 else depth - 1 - place
                turned = pltpu.roll(value, shift, 1) if shift else value
                packed = turned if packed is None else jnp.where(lane == where, turned, packed)
        own_edge[r, x] = packed

    def gather(r, x, q):
        step_x, step_y, _ = VELOCITY[q]
        value = ext[r, x + 1 - step_x, SLOT[q]]
        if step_y:
            side = 0 if step_y == 1 else sides - 1
            packed = edge[r, side, x + 1 - step_x]
            place = UP.index(q) if step_y == 1 else DOWN.index(q)
            shift = -place * step_y % depth
            turned = pltpu.roll(packed, shift, 1) if shift else packed
            value = jnp.where(lane == (0 if step_y == 1 else depth - 1), turned, value)
        return value

    def keep(t, x, moments):
        _, u, stress, heat, flux, omega, ease = moments
        for k, value in enumerate((*u, heat, *flux, omega, ease, *stress)):
            saved[t, x, k] = value

    def kept(t, x, whole):
        values = [saved[t, x, k] for k in range(15 if whole else 8)]
        return (
            None, tuple(values[:3]), tuple(values[9:15]) if whole else None, values[3],
            tuple(values[4:7]), values[7], values[8] if whole else None,
        )

    def planes(body, after=(), then=None, early=None):
        for r in after:
            for i in range(2):
                for copy in copies(r, i)[1]:
                    copy.wait_recv()

        if early is not None:
            start(early, 1)
            start(early, 0)

        def step(i, carry):
            for r in after:
                for copy in copies(r, i)[0]:
                    copy.wait_recv()
            body(plane(i))
            if then is not None:
                start(then, i)
            return carry

        lax.fori_loop(0, 2, step, 0)

    def first(x):
        solid = solid_ref[x] != 0
        slow = jnp.where(solid, 0.0, 1.0) / (1.0 + resist_ref[x])
        kappa = 1.0 / (0.5 + 0.4 * conduct_ref[x])
        fields[x, 0] = slow
        fields[x, 1] = kappa
        f = [flow_ref[q, x] for q in range(19)]
        g = [heat_ref[q, x] for q in range(7)]
        moments = state_moments(f, g, slow)
        keep(0, x, moments)
        leave(FORWARD_0, x, collide(f, g, solid, kappa, moments))

    for load in loads[:5]:
        load.wait()
    planes(first)
    pl.semaphore_wait(barrier, len(partners))
    start(FORWARD_0, 1)
    start(FORWARD_0, 0)

    def seed(x):
        weights = [flow_w_ref[k, x] for k in range(3)]
        heat = heat_w_ref[x]
        members = [None] * MEMBERS
        for q in range(MEMBERS):
            if q >= 19:
                members[OPPOSITE[q]] = heat
            elif q:
                value = None
                for weight, step in zip(weights, VELOCITY[q]):
                    if step:
                        term = weight if step == 1 else -weight
                        value = term if value is None else value + term
                members[OPPOSITE[q]] = value
        leave(SEED, x, members)

    for load in loads[5:]:
        load.wait()
    planes(seed)

    def second(x):
        solid, slow, kappa = solid_ref[x] != 0, fields[x, 0], fields[x, 1]
        state = [gather(FORWARD_0, x, q) for q in range(MEMBERS)]
        f, g = state[:19], state[19:]
        moments = state_moments(f, g, slow)
        keep(1, x, moments)
        leave(FORWARD_1, x, collide(f, g, solid, kappa, moments))

    planes(second, after=(FORWARD_0,), then=FORWARD_1, early=SEED)

    def reverse(r, x, moments, target):
        solid, slow, kappa = solid_ref[x] != 0, fields[x, 0], fields[x, 1]
        back = [
            jnp.zeros((height, depth), jnp.float32) if r == SEED and q == 0
            else gather(r, x, OPPOSITE[q])
            for q in range(MEMBERS)
        ]
        l, m = back[:19], back[19:]
        sums = adjoint_sums(l, m, jnp.where(solid, 0.0, 1.0))
        _, u, _, heat, flux, omega, _ = moments
        u_back, bent, resist, conduct = sensitivities(sums, u, heat, flux, omega, kappa)
        if r == SEED:
            resist_out[x] = resist
            conduct_out[x] = conduct
        elif target is not None:
            resist_out[x] += resist
            conduct_out[x] += conduct
        else:
            resist_out[x] = -(resist_out[x] + resist) / (1.0 + resist_ref[x])
            conduct_out[x] = (conduct_out[x] + conduct) * (-0.4 * kappa * kappa)
        if target is not None:
            out = collide_back(l, m, sums, moments, u_back, bent, solid, slow, kappa)
            leave(target, x, [out[OPPOSITE[q]] for q in range(MEMBERS)])

    def third(x):
        state = [gather(FORWARD_1, x, q) for q in range(MEMBERS)]
        reverse(SEED, x, state_moments(state[:19], state[19:], fields[x, 0]), BACK_2)

    planes(third, after=(SEED, FORWARD_1), then=BACK_2)
    planes(
        lambda x: reverse(BACK_2, x, kept(1, x, True), BACK_1), after=(BACK_2,), then=BACK_1
    )
    planes(lambda x: reverse(BACK_1, x, kept(0, x, False), None), after=(BACK_1,))

    for r in range(ROUNDS):
        for i in range(2):
            across, within = copies(r, i)
            for copy in across + within:
                copy.wait_send()


def on_device(gx, gy, flow, heat, flow_weight, heat_weight, resistance, conductivity, solid_mask):
    shape = resistance.shape
    width, height, depth = shape
    sides = 1 if gy == 2 else 2
    count = 1 + 2 * sides
    args = (flow, heat, resistance, conductivity, solid_mask, flow_weight, heat_weight)
    far = pl.BlockSpec(memory_space=pltpu.HBM)
    near = pl.BlockSpec(memory_space=pltpu.VMEM)
    found = pl.pallas_call(
        functools.partial(kernel, gx, gy),
        out_shape=jax.ShapeDtypeStruct((2,) + shape, jnp.float32),
        in_specs=[far] * len(args),
        out_specs=near,
        scratch_shapes=[pltpu.VMEM(a.shape, a.dtype) for a in args] + [
            pltpu.VMEM((ROUNDS, width + 2, MEMBERS, height, depth), jnp.float32),
            pltpu.VMEM((ROUNDS, width, height, depth), jnp.float32),
            pltpu.VMEM((ROUNDS, sides, width + 2, height, depth), jnp.float32),
            pltpu.VMEM((STEPS - 1, width, 15, height, depth), jnp.float32),
            pltpu.VMEM((width, 2, height, depth), jnp.float32),
            pltpu.SemaphoreType.DMA((len(args),)),
            pltpu.SemaphoreType.DMA((ROUNDS, 2, count)),
            pltpu.SemaphoreType.DMA((ROUNDS, 2, count)),
        ],
        compiler_params=pltpu.CompilerParams(
            collective_id=0, has_side_effects=True, vmem_limit_bytes=64 * 1024 * 1024
        ),
    )(*args)
    return found[0], found[1]


def solution(mesh):
    wide, flat = P(None, "gx", None, "gy"), P("gx", None, "gy")
    return jax.shard_map(
        functools.partial(on_device, mesh.shape["gx"], mesh.shape["gy"]),
        mesh=mesh,
        in_specs=(wide, wide, wide, flat, flat, flat, flat),
        out_specs=(flat, flat),
        check_vma=False,
    )
```

```python
import functools

import jax
import jax.numpy as jnp
from jax import lax
from jax.experimental import pallas as pl
from jax.experimental.pallas import tpu as pltpu
from jax.sharding import PartitionSpec as P

STEPS = 3
GHOST = 0.2
HEAT_GHOST = 0.4

FLOW = [
    (0, 0, 0), (1, 0, 0), (-1, 0, 0), (0, 1, 0), (0, -1, 0), (0, 0, 1), (0, 0, -1),
    (1, 1, 0), (-1, -1, 0), (1, -1, 0), (-1, 1, 0), (1, 0, 1), (-1, 0, -1),
    (1, 0, -1), (-1, 0, 1), (0, 1, 1), (0, -1, -1), (0, 1, -1), (0, -1, 1),
]
VELOCITY = FLOW + FLOW[:7]
MEMBERS = len(VELOCITY)
OPPOSITE = [0] + [q + 1 if q % 2 else q - 1 for q in range(1, 19)]
OPPOSITE = OPPOSITE + [19 + q for q in OPPOSITE[:7]]
ORDER = (
    [q for q in range(MEMBERS) if VELOCITY[q][0] == 1]
    + [q for q in range(MEMBERS) if VELOCITY[q][0] == -1]
    + [q for q in range(MEMBERS) if VELOCITY[q][0] == 0]
)
SLOT = [ORDER.index(q) for q in range(MEMBERS)]
FACE = sum(1 for q in range(MEMBERS) if VELOCITY[q][0] == 1)
UP = [q for q in range(MEMBERS) if VELOCITY[q][1] == 1]
DOWN = [q for q in range(MEMBERS) if VELOCITY[q][1] == -1]
ROUNDS = 5
PARTS = 3
FORWARD_0, SEED, FORWARD_1, BACK_2, BACK_1 = range(ROUNDS)
MESH = pl.DeviceIdType.MESH


def flow_moments(f):
    s = {q: f[q] + f[q + 1] for q in range(1, 19, 2)}
    d = {q: f[q] - f[q + 1] for q in range(1, 19, 2)}
    xy, xz, yz = s[7] + s[9], s[11] + s[13], s[15] + s[17]
    total = (f[0] + s[1] + s[3]) + (s[5] + xy) + (xz + yz)
    first = (
        (d[1] + d[7]) + (d[9] + d[11]) + d[13],
        (d[3] + d[7]) + (d[15] - d[9]) + d[17],
        (d[5] + d[11]) + (d[15] - d[13]) - d[17],
    )
    second = (
        s[1] + (xy + xz), s[3] + (xy + yz), s[5] + (xz + yz),
        s[7] - s[9], s[11] - s[13], s[15] - s[17],
    )
    return total, first, second


def spread(even, vector, tensor):
    x, y, z = vector
    xx, yy, zz, xy, xz, yz = tensor
    out = [even]

    def pair(e, o):
        out.append(e + o)
        out.append(e - o)

    ex, ey, ez = even + xx, even + yy, even + zz
    pair(ex, x)
    pair(ey, y)
    pair(ez, z)
    for e, cross, first, second in (
        (ex + yy, xy + xy, x, y), (ex + zz, xz + xz, x, z), (ey + zz, yz + yz, y, z)
    ):
        pair(e + cross, first + second)
        pair(e - cross, first - second)
    return out


def dot(a, b):
    return (a[0] * b[0] + a[1] * b[1]) + a[2] * b[2]


def state_moments(f, g, slow):
    density, momentum, second = flow_moments(f)
    third = density * (1.0 / 3.0)
    stress = tuple(m - third for m in second[:3]) + second[3:]
    u = tuple(slow * m for m in momentum)
    heat = (g[0] + (g[1] + g[2])) + ((g[3] + g[4]) + (g[5] + g[6]))
    flux = (g[1] - g[2], g[3] - g[4], g[5] - g[6])
    ease = jnp.exp(-2.0 * (heat - 1.0))
    omega = 1.0 / (0.5 + 0.3 * ease)
    return density, u, stress, heat, flux, omega, ease


def collide(f, g, solid, kappa, moments):
    density, u, stress, heat, flux, omega, _ = moments
    k_u, k_s = 4.5 * omega, 4.5 * (1.2 - omega)
    ku = tuple(k_u * m for m in u)
    tensor = (
        ku[0] * u[0] + k_s * stress[0], ku[1] * u[1] + k_s * stress[1],
        ku[2] * u[2] + k_s * stress[2], ku[0] * u[1] + k_s * stress[3],
        ku[0] * u[2] + k_s * stress[4], ku[1] * u[2] + k_s * stress[5],
    )
    even = 1.2 * density - (tensor[0] + tensor[1] + tensor[2]) * (1.0 / 3.0)
    vector = tuple(3.6 * m for m in u)
    w = 1.0 / 36.0
    relaxed = spread(
        w * even, tuple(w * m for m in vector), tuple(w * m for m in tensor)
    )
    out = []
    for q in range(19):
        scale = 12.0 if q == 0 else 2.0 if q < 7 else 1.0
        fluid = (relaxed[q] if scale == 1.0 else scale * relaxed[q]) - GHOST * f[q]
        out.append(jnp.where(solid, f[OPPOSITE[q]], fluid))
    sigma, pull = 1.4 - kappa, kappa * heat
    gate = tuple(0.5 * (pull * a + sigma * b) for a, b in zip(u, flux))
    base = (1.4 / 8.0) * heat
    out.append(2.0 * base - HEAT_GHOST * g[0])
    for axis in range(3):
        a, b = g[1 + 2 * axis], g[2 + 2 * axis]
        out.append((base + gate[axis]) - HEAT_GHOST * a)
        out.append((base - gate[axis]) - HEAT_GHOST * b)
    return out


def adjoint_sums(l, m, fluid):
    weighted = [12.0 * l[0]] + [2.0 * v for v in l[1:7]] + list(l[7:19])
    even, vector, tensor = flow_moments(weighted)
    scale = fluid * (1.0 / 36.0)
    even = scale * even
    vector = tuple(scale * v for v in vector)
    third = even * (1.0 / 3.0)
    tensor = tuple(scale * v - third for v in tensor[:3]) + tuple(scale * v for v in tensor[3:])
    gate = tuple(0.5 * (m[1 + 2 * k] - m[2 + 2 * k]) for k in range(3))
    return even, vector, tensor, gate


def sensitivities(sums, u, heat, flux, omega, kappa):
    _, vector, (xx, yy, zz, xy, xz, yz), gate = sums
    bent = (
        (xx * u[0] + xy * u[1]) + xz * u[2],
        (xy * u[0] + yy * u[1]) + yz * u[2],
        (xz * u[0] + yz * u[1]) + zz * u[2],
    )
    k_u, pull = 9.0 * omega, kappa * heat
    back = tuple(k_u * b + (3.6 * v + pull * e) for b, v, e in zip(bent, vector, gate))
    resist = dot(u, back)
    conduct = dot(gate, tuple(heat * a - b for a, b in zip(u, flux)))
    return back, bent, resist, conduct


def collide_back(l, m, sums, moments, back, bent, solid, slow, kappa):
    even, vector, tensor, gate = sums
    _, u, stress, heat, flux, omega, ease = moments
    xx, yy, zz, xy, xz, yz = tensor
    cross = xy * stress[3] + xz * stress[4] + yz * stress[5]
    inner = (xx * stress[0] + yy * stress[1]) + (zz * stress[2] + (cross + cross))
    omega_back = 4.5 * (dot(u, bent) - inner)
    k_s = 4.5 * (1.2 - omega)
    stress_back = tuple(k_s * t for t in tensor)
    density_back = 1.2 * even - (stress_back[0] + stress_back[1] + stress_back[2]) * (1.0 / 3.0)
    momentum_back = tuple(slow * b for b in back)
    smooth = spread(density_back, momentum_back, stress_back)
    out = []
    for q in range(19):
        out.append(jnp.where(solid, l[OPPOSITE[q]], -GHOST * l[q]) + smooth[q])
    moved = (m[0] + m[0] + (m[1] + m[2])) + ((m[3] + m[4]) + (m[5] + m[6]))
    heat_back = (1.4 / 8.0) * moved + kappa * dot(gate, u) + omega_back * (0.6 * ease) * (omega * omega)
    sigma = 1.4 - kappa
    flux_back = tuple(sigma * e for e in gate)
    out.append(heat_back - HEAT_GHOST * m[0])
    for axis in range(3):
        a, b = m[1 + 2 * axis], m[2 + 2 * axis]
        out.append((heat_back + flux_back[axis]) - HEAT_GHOST * a)
        out.append((heat_back - flux_back[axis]) - HEAT_GHOST * b)
    return out


def kernel(
    gx, gy, *refs
):
    whole, result, inputs = refs[:7], refs[7], refs[8:15]
    resist_out, conduct_out = result.at[0], result.at[1]
    flow_ref, heat_ref, resist_ref, conduct_ref, solid_ref, flow_w_ref, heat_w_ref = inputs
    ext, own_edge, edge, saved, fields, load_sem, send_sem, recv_sem = refs[15:]
    width, height, depth = resist_ref.shape
    sides = edge.shape[1]
    me_x, me_y = lax.axis_index("gx"), lax.axis_index("gy")
    right, left = lax.rem(me_x + 1, gx), lax.rem(me_x + gx - 1, gx)
    up, down = lax.rem(me_y + 1, gy), lax.rem(me_y + gy - 1, gy)
    columns = [(up, 0)] if sides == 1 else [(up, 0), (down, 1)]

    loads = [
        pltpu.make_async_copy(src, dst, load_sem.at[k])
        for k, (src, dst) in enumerate(zip(whole, inputs))
    ]
    barrier = pltpu.get_barrier_semaphore()
    partners = [(right, me_y), (left, me_y)]
    for y, _ in columns:
        partners += [(me_x, y), (right, y), (left, y)]
    for partner in partners:
        pl.semaphore_signal(barrier, inc=1, device_id=partner, device_id_type=MESH)
    for load in loads:
        load.start()

    lane = lax.broadcasted_iota(jnp.int32, (height, depth), 1)

    def plane(i):
        return lax.rem(me_x + 1 + i, 2)

    def copies(r, i):
        x = plane(i)
        upper = x == width - 1
        beside = jnp.where(upper, right, left)
        halo = jnp.where(upper, 0, width + 1)
        group = jnp.where(upper, 0, FACE)

        def remote(k, src, dst, device):
            return pltpu.make_async_remote_copy(
                src_ref=src, dst_ref=dst,
                send_sem=send_sem.at[r, i, k], recv_sem=recv_sem.at[r, i, k],
                device_id=device, device_id_type=MESH,
            )

        across, within = [], []
        for y, side in columns:
            k = PARTS + 2 * side
            across.append(remote(k, own_edge.at[r, x], edge.at[r, side, halo], (beside, y)))
            within.append(remote(k + 1, own_edge.at[r, x], edge.at[r, side, x + 1], (me_x, y)))
        for k in range(PARTS):
            part = pl.ds(group + k * (FACE // PARTS), FACE // PARTS)
            across.append(
                remote(k, ext.at[r, x + 1, part], ext.at[r, halo, part], (beside, me_y))
            )
        return across, within

    def start(r, i):
        across, within = copies(r, i)
        for copy in across + within:
            copy.start()

    def leave(r, x, members):
        packed = None
        for q in range(MEMBERS):
            if members[q] is None:
                continue
            value = members[q]
            _, step_y, step_z = VELOCITY[q]
            if step_z:
                value = pltpu.roll(value, step_z % height, 0)
            if step_y:
                value = pltpu.roll(value, step_y % depth, 1)
            ext[r, x + 1, SLOT[q]] = value
            if step_y:
                place = UP.index(q) if step_y == 1 else DOWN.index(q)
                shift = place * step_y % depth
                where = place if step_y == 1 else depth - 1 - place
                turned = pltpu.roll(value, shift, 1) if shift else value
                packed = turned if packed is None else jnp.where(lane == where, turned, packed)
        own_edge[r, x] = packed

    def gather(r, x, q):
        step_x, step_y, _ = VELOCITY[q]
        value = ext[r, x + 1 - step_x, SLOT[q]]
        if step_y:
            side = 0 if step_y == 1 else sides - 1
            packed = edge[r, side, x + 1 - step_x]
            place = UP.index(q) if step_y == 1 else DOWN.index(q)
            shift = -place * step_y % depth
            turned = pltpu.roll(packed, shift, 1) if shift else packed
            value = jnp.where(lane == (0 if step_y == 1 else depth - 1), turned, value)
        return value

    def keep(t, x, moments):
        _, u, stress, heat, flux, omega, ease = moments
        for k, value in enumerate((*u, heat, *flux, omega, ease, *stress)):
            saved[t, x, k] = value

    def kept(t, x, whole):
        values = [saved[t, x, k] for k in range(15 if whole else 8)]
        return (
            None, tuple(values[:3]), tuple(values[9:15]) if whole else None, values[3],
            tuple(values[4:7]), values[7], values[8] if whole else None,
        )

    def planes(body, after=(), then=None, early=None):
        for r in after:
            for i in range(2):
                for copy in copies(r, i)[1]:
                    copy.wait_recv()

        if early is not None:
            start(early, 1)
            start(early, 0)

        def step(i, carry):
            for r in after:
                for copy in copies(r, i)[0]:
                    copy.wait_recv()
            body(plane(i))
            if then is not None:
                start(then, i)
            return carry

        lax.fori_loop(0, 2, step, 0)

    def first(x):
        solid = solid_ref[x] != 0
        slow = jnp.where(solid, 0.0, 1.0) / (1.0 + resist_ref[x])
        kappa = 1.0 / (0.5 + 0.4 * conduct_ref[x])
        fields[x, 0] = slow
        fields[x, 1] = kappa
        f = [flow_ref[q, x] for q in range(19)]
        g = [heat_ref[q, x] for q in range(7)]
        moments = state_moments(f, g, slow)
        keep(0, x, moments)
        leave(FORWARD_0, x, collide(f, g, solid, kappa, moments))

    for load in loads[:5]:
        load.wait()
    first(plane(1))
    pl.semaphore_wait(barrier, len(partners))
    start(FORWARD_0, 1)
    first(plane(0))
    start(FORWARD_0, 0)

    def seed(x):
        weights = [flow_w_ref[k, x] for k in range(3)]
        heat = heat_w_ref[x]
        members = [None] * MEMBERS
        for q in range(MEMBERS):
            if q >= 19:
                members[OPPOSITE[q]] = heat
            elif q:
                value = None
                for weight, step in zip(weights, VELOCITY[q]):
                    if step:
                        term = weight if step == 1 else -weight
                        value = term if value is None else value + term
                members[OPPOSITE[q]] = value
        leave(SEED, x, members)

    for load in loads[5:]:
        load.wait()
    planes(seed)

    def second(x):
        solid, slow, kappa = solid_ref[x] != 0, fields[x, 0], fields[x, 1]
        state = [gather(FORWARD_0, x, q) for q in range(MEMBERS)]
        f, g = state[:19], state[19:]
        moments = state_moments(f, g, slow)
        keep(1, x, moments)
        leave(FORWARD_1, x, collide(f, g, solid, kappa, moments))

    planes(second, after=(FORWARD_0,), then=FORWARD_1, early=SEED)

    def reverse(r, x, moments, target):
        solid, slow, kappa = solid_ref[x] != 0, fields[x, 0], fields[x, 1]
        back = [
            jnp.zeros((height, depth), jnp.float32) if r == SEED and q == 0
            else gather(r, x, OPPOSITE[q])
            for q in range(MEMBERS)
        ]
        l, m = back[:19], back[19:]
        sums = adjoint_sums(l, m, jnp.where(solid, 0.0, 1.0))
        _, u, _, heat, flux, omega, _ = moments
        u_back, bent, resist, conduct = sensitivities(sums, u, heat, flux, omega, kappa)
        if r == SEED:
            resist_out[x] = resist
            conduct_out[x] = conduct
        elif target is not None:
            resist_out[x] += resist
            conduct_out[x] += conduct
        else:
            resist_out[x] = -(resist_out[x] + resist) / (1.0 + resist_ref[x])
            conduct_out[x] = (conduct_out[x] + conduct) * (-0.4 * kappa * kappa)
        if target is not None:
            out = collide_back(l, m, sums, moments, u_back, bent, solid, slow, kappa)
            leave(target, x, [out[OPPOSITE[q]] for q in range(MEMBERS)])

    def third(x):
        state = [gather(FORWARD_1, x, q) for q in range(MEMBERS)]
        reverse(SEED, x, state_moments(state[:19], state[19:], fields[x, 0]), BACK_2)

    planes(third, after=(SEED, FORWARD_1), then=BACK_2)
    planes(
        lambda x: reverse(BACK_2, x, kept(1, x, True), BACK_1), after=(BACK_2,), then=BACK_1
    )
    planes(lambda x: reverse(BACK_1, x, kept(0, x, False), None), after=(BACK_1,))

    for r in range(ROUNDS):
        for i in range(2):
            across, within = copies(r, i)
            for copy in across + within:
                copy.wait_send()


def on_device(gx, gy, flow, heat, flow_weight, heat_weight, resistance, conductivity, solid_mask):
    shape = resistance.shape
    width, height, depth = shape
    sides = 1 if gy == 2 else 2
    count = PARTS + 2 * sides
    args = (flow, heat, resistance, conductivity, solid_mask, flow_weight, heat_weight)
    far = pl.BlockSpec(memory_space=pltpu.HBM)
    near = pl.BlockSpec(memory_space=pltpu.VMEM)
    found = pl.pallas_call(
        functools.partial(kernel, gx, gy),
        out_shape=jax.ShapeDtypeStruct((2,) + shape, jnp.float32),
        in_specs=[far] * len(args),
        out_specs=near,
        scratch_shapes=[pltpu.VMEM(a.shape, a.dtype) for a in args] + [
            pltpu.VMEM((ROUNDS, width + 2, MEMBERS, height, depth), jnp.float32),
            pltpu.VMEM((ROUNDS, width, height, depth), jnp.float32),
            pltpu.VMEM((ROUNDS, sides, width + 2, height, depth), jnp.float32),
            pltpu.VMEM((STEPS - 1, width, 15, height, depth), jnp.float32),
            pltpu.VMEM((width, 2, height, depth), jnp.float32),
            pltpu.SemaphoreType.DMA((len(args),)),
            pltpu.SemaphoreType.DMA((ROUNDS, 2, count)),
            pltpu.SemaphoreType.DMA((ROUNDS, 2, count)),
        ],
        compiler_params=pltpu.CompilerParams(
            collective_id=0, has_side_effects=True, vmem_limit_bytes=64 * 1024 * 1024
        ),
    )(*args)
    return found[0], found[1]


def solution(mesh):
    wide, flat = P(None, "gx", None, "gy"), P("gx", None, "gy")
    return jax.shard_map(
        functools.partial(on_device, mesh.shape["gx"], mesh.shape["gy"]),
        mesh=mesh,
        in_specs=(wide, wide, wide, flat, flat, flat, flat),
        out_specs=(flat, flat),
        check_vma=False,
    )
```

```python
import functools

import jax
import jax.numpy as jnp
from jax import lax
from jax.experimental import pallas as pl
from jax.experimental.pallas import tpu as pltpu
from jax.sharding import PartitionSpec as P

STEPS = 3
GHOST = 0.2
HEAT_GHOST = 0.4

FLOW = [
    (0, 0, 0), (1, 0, 0), (-1, 0, 0), (0, 1, 0), (0, -1, 0), (0, 0, 1), (0, 0, -1),
    (1, 1, 0), (-1, -1, 0), (1, -1, 0), (-1, 1, 0), (1, 0, 1), (-1, 0, -1),
    (1, 0, -1), (-1, 0, 1), (0, 1, 1), (0, -1, -1), (0, 1, -1), (0, -1, 1),
]
VELOCITY = FLOW + FLOW[:7]
MEMBERS = len(VELOCITY)
OPPOSITE = [0] + [q + 1 if q % 2 else q - 1 for q in range(1, 19)]
OPPOSITE = OPPOSITE + [19 + q for q in OPPOSITE[:7]]
ORDER = (
    [q for q in range(MEMBERS) if VELOCITY[q][0] == 1]
    + [q for q in range(MEMBERS) if VELOCITY[q][0] == -1]
    + [q for q in range(MEMBERS) if VELOCITY[q][0] == 0]
)
SLOT = [ORDER.index(q) for q in range(MEMBERS)]
FACE = sum(1 for q in range(MEMBERS) if VELOCITY[q][0] == 1)
UP = [q for q in range(MEMBERS) if VELOCITY[q][1] == 1]
DOWN = [q for q in range(MEMBERS) if VELOCITY[q][1] == -1]
ROUNDS = 5
PARTS = 1
FORWARD_0, SEED, FORWARD_1, BACK_2, BACK_1 = range(ROUNDS)
MESH = pl.DeviceIdType.MESH


def flow_moments(f):
    s = {q: f[q] + f[q + 1] for q in range(1, 19, 2)}
    d = {q: f[q] - f[q + 1] for q in range(1, 19, 2)}
    xy, xz, yz = s[7] + s[9], s[11] + s[13], s[15] + s[17]
    total = (f[0] + s[1] + s[3]) + (s[5] + xy) + (xz + yz)
    first = (
        (d[1] + d[7]) + (d[9] + d[11]) + d[13],
        (d[3] + d[7]) + (d[15] - d[9]) + d[17],
        (d[5] + d[11]) + (d[15] - d[13]) - d[17],
    )
    second = (
        s[1] + (xy + xz), s[3] + (xy + yz), s[5] + (xz + yz),
        s[7] - s[9], s[11] - s[13], s[15] - s[17],
    )
    return total, first, second


def spread(even, vector, tensor):
    x, y, z = vector
    xx, yy, zz, xy, xz, yz = tensor
    out = [even]

    def pair(e, o):
        out.append(e + o)
        out.append(e - o)

    ex, ey, ez = even + xx, even + yy, even + zz
    pair(ex, x)
    pair(ey, y)
    pair(ez, z)
    for e, cross, first, second in (
        (ex + yy, xy + xy, x, y), (ex + zz, xz + xz, x, z), (ey + zz, yz + yz, y, z)
    ):
        pair(e + cross, first + second)
        pair(e - cross, first - second)
    return out


def dot(a, b):
    return (a[0] * b[0] + a[1] * b[1]) + a[2] * b[2]


def state_moments(f, g, slow):
    density, momentum, second = flow_moments(f)
    third = density * (1.0 / 3.0)
    stress = tuple(m - third for m in second[:3]) + second[3:]
    u = tuple(slow * m for m in momentum)
    heat = (g[0] + (g[1] + g[2])) + ((g[3] + g[4]) + (g[5] + g[6]))
    flux = (g[1] - g[2], g[3] - g[4], g[5] - g[6])
    ease = jnp.exp(-2.0 * (heat - 1.0))
    omega = 1.0 / (0.5 + 0.3 * ease)
    return density, u, stress, heat, flux, omega, ease


def collide(f, g, solid, kappa, moments):
    density, u, stress, heat, flux, omega, _ = moments
    k_u, k_s = 4.5 * omega, 4.5 * (1.2 - omega)
    ku = tuple(k_u * m for m in u)
    tensor = (
        ku[0] * u[0] + k_s * stress[0], ku[1] * u[1] + k_s * stress[1],
        ku[2] * u[2] + k_s * stress[2], ku[0] * u[1] + k_s * stress[3],
        ku[0] * u[2] + k_s * stress[4], ku[1] * u[2] + k_s * stress[5],
    )
    even = 1.2 * density - (tensor[0] + tensor[1] + tensor[2]) * (1.0 / 3.0)
    vector = tuple(3.6 * m for m in u)
    w = 1.0 / 36.0
    relaxed = spread(
        w * even, tuple(w * m for m in vector), tuple(w * m for m in tensor)
    )
    out = []
    for q in range(19):
        scale = 12.0 if q == 0 else 2.0 if q < 7 else 1.0
        fluid = (relaxed[q] if scale == 1.0 else scale * relaxed[q]) - GHOST * f[q]
        out.append(jnp.where(solid, f[OPPOSITE[q]], fluid))
    sigma, pull = 1.4 - kappa, kappa * heat
    gate = tuple(0.5 * (pull * a + sigma * b) for a, b in zip(u, flux))
    base = (1.4 / 8.0) * heat
    out.append(2.0 * base - HEAT_GHOST * g[0])
    for axis in range(3):
        a, b = g[1 + 2 * axis], g[2 + 2 * axis]
        out.append((base + gate[axis]) - HEAT_GHOST * a)
        out.append((base - gate[axis]) - HEAT_GHOST * b)
    return out


def adjoint_sums(l, m, fluid):
    weighted = [12.0 * l[0]] + [2.0 * v for v in l[1:7]] + list(l[7:19])
    even, vector, tensor = flow_moments(weighted)
    scale = fluid * (1.0 / 36.0)
    even = scale * even
    vector = tuple(scale * v for v in vector)
    third = even * (1.0 / 3.0)
    tensor = tuple(scale * v - third for v in tensor[:3]) + tuple(scale * v for v in tensor[3:])
    gate = tuple(0.5 * (m[1 + 2 * k] - m[2 + 2 * k]) for k in range(3))
    return even, vector, tensor, gate


def sensitivities(sums, u, heat, flux, omega, kappa):
    _, vector, (xx, yy, zz, xy, xz, yz), gate = sums
    bent = (
        (xx * u[0] + xy * u[1]) + xz * u[2],
        (xy * u[0] + yy * u[1]) + yz * u[2],
        (xz * u[0] + yz * u[1]) + zz * u[2],
    )
    k_u, pull = 9.0 * omega, kappa * heat
    back = tuple(k_u * b + (3.6 * v + pull * e) for b, v, e in zip(bent, vector, gate))
    resist = dot(u, back)
    conduct = dot(gate, tuple(heat * a - b for a, b in zip(u, flux)))
    return back, bent, resist, conduct


def collide_back(l, m, sums, moments, back, bent, solid, slow, kappa):
    even, vector, tensor, gate = sums
    _, u, stress, heat, flux, omega, ease = moments
    xx, yy, zz, xy, xz, yz = tensor
    cross = xy * stress[3] + xz * stress[4] + yz * stress[5]
    inner = (xx * stress[0] + yy * stress[1]) + (zz * stress[2] + (cross + cross))
    omega_back = 4.5 * (dot(u, bent) - inner)
    k_s = 4.5 * (1.2 - omega)
    stress_back = tuple(k_s * t for t in tensor)
    density_back = 1.2 * even - (stress_back[0] + stress_back[1] + stress_back[2]) * (1.0 / 3.0)
    momentum_back = tuple(slow * b for b in back)
    smooth = spread(density_back, momentum_back, stress_back)
    out = []
    for q in range(19):
        out.append(jnp.where(solid, l[OPPOSITE[q]], -GHOST * l[q]) + smooth[q])
    moved = (m[0] + m[0] + (m[1] + m[2])) + ((m[3] + m[4]) + (m[5] + m[6]))
    heat_back = (1.4 / 8.0) * moved + kappa * dot(gate, u) + omega_back * (0.6 * ease) * (omega * omega)
    sigma = 1.4 - kappa
    flux_back = tuple(sigma * e for e in gate)
    out.append(heat_back - HEAT_GHOST * m[0])
    for axis in range(3):
        a, b = m[1 + 2 * axis], m[2 + 2 * axis]
        out.append((heat_back + flux_back[axis]) - HEAT_GHOST * a)
        out.append((heat_back - flux_back[axis]) - HEAT_GHOST * b)
    return out


def kernel(
    gx, gy, *refs
):
    whole, result, inputs = refs[:7], refs[7], refs[8:15]
    resist_out, conduct_out = result.at[0], result.at[1]
    flow_ref, heat_ref, resist_ref, conduct_ref, solid_ref, flow_w_ref, heat_w_ref = inputs
    ext, corner, own_edge, edge, saved, fields, load_sem, send_sem, recv_sem = refs[15:]
    width, height, depth = resist_ref.shape
    sides = edge.shape[1]
    me_x, me_y = lax.axis_index("gx"), lax.axis_index("gy")
    right, left = lax.rem(me_x + 1, gx), lax.rem(me_x + gx - 1, gx)
    up, down = lax.rem(me_y + 1, gy), lax.rem(me_y + gy - 1, gy)
    columns = [(up, 0)] if sides == 1 else [(up, 0), (down, 1)]

    loads = [
        pltpu.make_async_copy(src, dst, load_sem.at[k])
        for k, (src, dst) in enumerate(zip(whole, inputs))
    ]
    barrier = pltpu.get_barrier_semaphore()
    partners = [(right, me_y), (left, me_y)]
    for y, _ in columns:
        partners += [(me_x, y), (right, y), (left, y)]
    for partner in partners:
        pl.semaphore_signal(barrier, inc=1, device_id=partner, device_id_type=MESH)
    for load in loads:
        load.start()

    lane = lax.broadcasted_iota(jnp.int32, (height, depth), 1)

    def plane(i):
        return lax.rem(me_x + 1 + i, 2)

    def copies(r, i):
        x = plane(i)
        upper = x == width - 1
        beside = jnp.where(upper, right, left)
        halo = jnp.where(upper, 0, width + 1)
        group = jnp.where(upper, 0, FACE)

        def remote(k, src, dst, device):
            return pltpu.make_async_remote_copy(
                src_ref=src, dst_ref=dst,
                send_sem=send_sem.at[r, i, k], recv_sem=recv_sem.at[r, i, k],
                device_id=device, device_id_type=MESH,
            )

        across, within = [], []
        for y, side in columns:
            k = PARTS + 2 * side
            across.append(remote(k, corner.at[r, x], edge.at[r, side, halo], (beside, y)))
            within.append(remote(k + 1, own_edge.at[r, x], edge.at[r, side, x + 1], (me_x, y)))
        for k in range(PARTS):
            part = pl.ds(group + k * (FACE // PARTS), FACE // PARTS)
            across.append(
                remote(k, ext.at[r, x + 1, part], ext.at[r, halo, part], (beside, me_y))
            )
        return across, within

    def start(r, i, which):
        for copy in copies(r, i)[which]:
            copy.start()

    def leave(r, x, members, send=None, entry=False):
        packed = None
        for crossing in (True, False):
            for q in range(MEMBERS):
                step_x, step_y, step_z = VELOCITY[q]
                if members[q] is None or bool(step_x) != crossing:
                    continue
                value = members[q]
                if step_z:
                    value = pltpu.roll(value, step_z % height, 0)
                if step_y:
                    value = pltpu.roll(value, step_y % depth, 1)
                ext[r, x + 1, SLOT[q]] = value
                if step_y:
                    place = UP.index(q) if step_y == 1 else DOWN.index(q)
                    shift = place * step_y % depth
                    where = place if step_y == 1 else depth - 1 - place
                    turned = pltpu.roll(value, shift, 1) if shift else value
                    packed = turned if packed is None else jnp.where(lane == where, turned, packed)
            if crossing:
                corner[r, x] = packed
                if entry:
                    pl.semaphore_wait(barrier, len(partners))
                if send is not None:
                    start(r, send, 0)
            else:
                own_edge[r, x] = packed
                if send is not None:
                    start(r, send, 1)

    def gather(r, x, q):
        step_x, step_y, _ = VELOCITY[q]
        value = ext[r, x + 1 - step_x, SLOT[q]]
        if step_y:
            side = 0 if step_y == 1 else sides - 1
            packed = edge[r, side, x + 1 - step_x]
            place = UP.index(q) if step_y == 1 else DOWN.index(q)
            shift = -place * step_y % depth
            turned = pltpu.roll(packed, shift, 1) if shift else packed
            value = jnp.where(lane == (0 if step_y == 1 else depth - 1), turned, value)
        return value

    def keep(t, x, moments):
        _, u, stress, heat, flux, omega, ease = moments
        for k, value in enumerate((*u, heat, *flux, omega, ease, *stress)):
            saved[t, x, k] = value

    def kept(t, x, whole):
        values = [saved[t, x, k] for k in range(15 if whole else 8)]
        return (
            None, tuple(values[:3]), tuple(values[9:15]) if whole else None, values[3],
            tuple(values[4:7]), values[7], values[8] if whole else None,
        )

    def planes(body, after=(), early=None):
        for r in after:
            for i in range(2):
                for copy in copies(r, i)[1]:
                    copy.wait_recv()

        if early is not None:
            for i in (1, 0):
                for which in range(2):
                    start(early, i, which)

        def step(i, carry):
            for r in after:
                for copy in copies(r, i)[0]:
                    copy.wait_recv()
            body(plane(i), i)
            return carry

        lax.fori_loop(0, 2, step, 0)

    def first(x, i):
        solid = solid_ref[x] != 0
        slow = jnp.where(solid, 0.0, 1.0) / (1.0 + resist_ref[x])
        kappa = 1.0 / (0.5 + 0.4 * conduct_ref[x])
        fields[x, 0] = slow
        fields[x, 1] = kappa
        f = [flow_ref[q, x] for q in range(19)]
        g = [heat_ref[q, x] for q in range(7)]
        moments = state_moments(f, g, slow)
        keep(0, x, moments)
        leave(FORWARD_0, x, collide(f, g, solid, kappa, moments), i, entry=i == 1)

    for load in loads[:5]:
        load.wait()
    first(plane(1), 1)
    first(plane(0), 0)

    def seed(x, _):
        weights = [flow_w_ref[k, x] for k in range(3)]
        heat = heat_w_ref[x]
        members = [None] * MEMBERS
        for q in range(MEMBERS):
            if q >= 19:
                members[OPPOSITE[q]] = heat
            elif q:
                value = None
                for weight, step in zip(weights, VELOCITY[q]):
                    if step:
                        term = weight if step == 1 else -weight
                        value = term if value is None else value + term
                members[OPPOSITE[q]] = value
        leave(SEED, x, members)

    for load in loads[5:]:
        load.wait()
    planes(seed)

    def second(x, i):
        solid, slow, kappa = solid_ref[x] != 0, fields[x, 0], fields[x, 1]
        state = [gather(FORWARD_0, x, q) for q in range(MEMBERS)]
        f, g = state[:19], state[19:]
        moments = state_moments(f, g, slow)
        keep(1, x, moments)
        leave(FORWARD_1, x, collide(f, g, solid, kappa, moments), i)

    planes(second, after=(FORWARD_0,), early=SEED)

    def reverse(r, x, i, moments, target):
        solid, slow, kappa = solid_ref[x] != 0, fields[x, 0], fields[x, 1]
        back = [
            jnp.zeros((height, depth), jnp.float32) if r == SEED and q == 0
            else gather(r, x, OPPOSITE[q])
            for q in range(MEMBERS)
        ]
        l, m = back[:19], back[19:]
        sums = adjoint_sums(l, m, jnp.where(solid, 0.0, 1.0))
        _, u, _, heat, flux, omega, _ = moments
        u_back, bent, resist, conduct = sensitivities(sums, u, heat, flux, omega, kappa)
        if r == SEED:
            resist_out[x] = resist
            conduct_out[x] = conduct
        elif target is not None:
            resist_out[x] += resist
            conduct_out[x] += conduct
        else:
            resist_out[x] = -(resist_out[x] + resist) / (1.0 + resist_ref[x])
            conduct_out[x] = (conduct_out[x] + conduct) * (-0.4 * kappa * kappa)
        if target is not None:
            out = collide_back(l, m, sums, moments, u_back, bent, solid, slow, kappa)
            leave(target, x, [out[OPPOSITE[q]] for q in range(MEMBERS)], i)

    def third(x, i):
        state = [gather(FORWARD_1, x, q) for q in range(MEMBERS)]
        reverse(SEED, x, i, state_moments(state[:19], state[19:], fields[x, 0]), BACK_2)

    planes(third, after=(SEED, FORWARD_1))
    planes(lambda x, i: reverse(BACK_2, x, i, kept(1, x, True), BACK_1), after=(BACK_2,))
    planes(lambda x, i: reverse(BACK_1, x, i, kept(0, x, False), None), after=(BACK_1,))

    for r in range(ROUNDS):
        for i in range(2):
            across, within = copies(r, i)
            for copy in across + within:
                copy.wait_send()


def on_device(gx, gy, flow, heat, flow_weight, heat_weight, resistance, conductivity, solid_mask):
    shape = resistance.shape
    width, height, depth = shape
    sides = 1 if gy == 2 else 2
    count = PARTS + 2 * sides
    args = (flow, heat, resistance, conductivity, solid_mask, flow_weight, heat_weight)
    far = pl.BlockSpec(memory_space=pltpu.HBM)
    near = pl.BlockSpec(memory_space=pltpu.VMEM)
    found = pl.pallas_call(
        functools.partial(kernel, gx, gy),
        out_shape=jax.ShapeDtypeStruct((2,) + shape, jnp.float32),
        in_specs=[far] * len(args),
        out_specs=near,
        scratch_shapes=[pltpu.VMEM(a.shape, a.dtype) for a in args] + [
            pltpu.VMEM((ROUNDS, width + 2, MEMBERS, height, depth), jnp.float32),
            pltpu.VMEM((ROUNDS, width, height, depth), jnp.float32),
            pltpu.VMEM((ROUNDS, width, height, depth), jnp.float32),
            pltpu.VMEM((ROUNDS, sides, width + 2, height, depth), jnp.float32),
            pltpu.VMEM((STEPS - 1, width, 15, height, depth), jnp.float32),
            pltpu.VMEM((width, 2, height, depth), jnp.float32),
            pltpu.SemaphoreType.DMA((len(args),)),
            pltpu.SemaphoreType.DMA((ROUNDS, 2, count)),
            pltpu.SemaphoreType.DMA((ROUNDS, 2, count)),
        ],
        compiler_params=pltpu.CompilerParams(
            collective_id=0, has_side_effects=True, vmem_limit_bytes=64 * 1024 * 1024
        ),
    )(*args)
    return found[0], found[1]


def solution(mesh):
    wide, flat = P(None, "gx", None, "gy"), P("gx", None, "gy")
    return jax.shard_map(
        functools.partial(on_device, mesh.shape["gx"], mesh.shape["gy"]),
        mesh=mesh,
        in_specs=(wide, wide, wide, flat, flat, flat, flat),
        out_specs=(flat, flat),
        check_vma=False,
    )
```
